256 devices in a mesh: qrow: 8 (over x_hi, y), kcol: 32 (over z, x_lo, core).
Axes of the slice: x: 4 (x_hi: 2, x_lo: 2; x = x_hi * 2 + x_lo), y: 4, z: 8, core: 2. Of those that a mesh axis runs over, the one named last changes fastest.
Arguments:
- homolog_source_features: bfloat16 [16, 768, 256], P(None, ('qrow', 'kcol')), may hold values from -6 to 6
- homolog_target_features: bfloat16 [16, 2048, 256], P('qrow', 'kcol'), may hold values from -6 to 6
- first_factor_matrix: bfloat16 [256, 32], replicated, may hold values from -0.375 to 0.375
- second_factor_matrix: bfloat16 [256, 32], replicated, may hold values from -0.375 to 0.375
- output_weight: bfloat16 [1024, 128], replicated, may hold values from -0.1875 to 0.1875
- output_bias: float32 [128], replicated, may hold values from -4 to 4
- pair_cotangent: bfloat16 [768, 2048, 128], P('qrow', 'kcol'), may hold values from -6 to 6
Outputs:
- pair_update: bfloat16 [768, 2048, 128], P('qrow', 'kcol')
- grad_rows: bfloat16 [16, 768, 256], P(None, ('qrow', 'kcol'))
- grad_cols: bfloat16 [16, 2048, 256], P('qrow', 'kcol')
- grad_w_out: float32 [1024, 128], replicated
- grad_b_out: float32 [128], replicated
- grad_w_left: float32 [256, 32], replicated
- grad_w_right: float32 [256, 32], replicated
The draws below stay inside these ranges and needn't reach their ends.
All inputs are finite; a program needn't handle non-finite values.
Results may differ from the reference program's by a relative error of at most 0.033.
Values may be sent and summed in bfloat16 or wider, within the bound.
A program may use at most 128 MiB of HBM per device.

```python
import jax
import jax.numpy as jnp
from jax import lax

FEATURE_DEPTH = 256
PROJECTED_WIDTH = 32
ZPLANE_FEATURES = 128
HOMOLOG_TOTAL = 16
SOURCE_POSITIONS = 768
TARGET_POSITIONS = 2048


def spiked(result, stream_key, source, target, parts, factor):
    owner, partner = [(jnp.arange(result.shape[axis_at]) // (result.shape[axis_at] // parts)).reshape([-1 if axis == axis_at else 1 for axis in range(result.ndim)]) for axis_at in (source, target)]
    chosen = jax.random.permutation(stream_key, parts)[partner]
    strong = (owner == chosen) | (owner == (partner + parts // 2) % parts)
    return jnp.where(strong, factor * result, result)


def shard_levels(stream_key, extent, split, low, high):
    factor_of = 1.0
    for position, parts in split:
        heights = jax.random.uniform(jax.random.fold_in(jax.random.fold_in(stream_key, 6), position), (parts,), jnp.float32, low / len(split), high / len(split))
        factor_of = factor_of * jnp.repeat(jnp.exp(heights), extent[position] // parts).reshape((-1,) + (1,) * (len(extent) - 1 - position))
    return factor_of


def noise(stream_key, shape, spread, reach, cuts=(), kind=jnp.bfloat16):
    result = jax.random.normal(stream_key, shape, jnp.float32) * spread
    if len(cuts) > 0:
        result = shard_levels(stream_key, shape, cuts, -0.22, 0.18) * result
    return jnp.clip(result, min=-reach, max=reach).astype(kind)


def gaussian_with(rng, shape, width, bound, cuts, heavy, held_as=jnp.bfloat16):
    array = width * jax.random.normal(rng, shape, jnp.float32)
    if cuts:
        array = array * shard_levels(rng, shape, cuts, -0.22, 0.18)
    return jnp.clip(spiked(array, jax.random.fold_in(rng, 3), *heavy), -bound, bound).astype(held_as)


def setup_inputs(seed: int = 0) -> dict:
    key_of = jax.random.split(jax.random.key(seed), 8)
    homolog_source_features = noise(key_of[0], (HOMOLOG_TOTAL, SOURCE_POSITIONS, FEATURE_DEPTH), 1.0, 6.0, ((1, 256),))
    homolog_target_features = noise(key_of[1], (HOMOLOG_TOTAL, TARGET_POSITIONS, FEATURE_DEPTH), 1.0, 6.0, ((0, 8), (1, 32)))
    first_factor_matrix = noise(key_of[2], (FEATURE_DEPTH, PROJECTED_WIDTH), FEATURE_DEPTH ** -0.5, 0.375)
    second_factor_matrix = noise(key_of[3], (FEATURE_DEPTH, PROJECTED_WIDTH), FEATURE_DEPTH ** -0.5, 0.375)
    output_weight = noise(key_of[4], (PROJECTED_WIDTH * PROJECTED_WIDTH, ZPLANE_FEATURES), (PROJECTED_WIDTH * PROJECTED_WIDTH) ** -0.5, 0.1875)
    output_bias = noise(key_of[5], (ZPLANE_FEATURES,), 1.0, 4.0, (), jnp.float32)
    pair_cotangent = gaussian_with(key_of[6], (SOURCE_POSITIONS, TARGET_POSITIONS, ZPLANE_FEATURES), 1.0, 6.0, ((0, 8), (1, 32)), (1, 0, 32, 2.75))
    return {"homolog_source_features": homolog_source_features, "homolog_target_features": homolog_target_features, "first_factor_matrix": first_factor_matrix, "second_factor_matrix": second_factor_matrix, "output_weight": output_weight, "output_bias": output_bias, "pair_cotangent": pair_cotangent}


def layer_normalize(x):
    values = x.astype(jnp.float32)
    center = values - lax.optimization_barrier(jnp.mean(values, axis=-1, keepdims=True))
    inverse = lax.rsqrt(lax.optimization_barrier(jnp.mean(center * center, axis=-1, keepdims=True)) + 1e-05)
    return (center * inverse, inverse)

def norm_back(grad_norm, normed, inverse):
    first = lax.optimization_barrier(jnp.mean(grad_norm, axis=-1, keepdims=True))
    second = lax.optimization_barrier(jnp.mean(grad_norm * normed, axis=-1, keepdims=True))
    return (inverse * (grad_norm - first - normed * second)).astype(jnp.bfloat16)

def reference(homolog_source_features, homolog_target_features, first_factor_matrix, second_factor_matrix, output_weight, output_bias, pair_cotangent):
    centered_query_rows, inverse_std_rows = layer_normalize(homolog_source_features)
    centered_key_columns, inverse_std_columns = layer_normalize(homolog_target_features)
    ln_rows = centered_query_rows.astype(jnp.bfloat16)
    ln_cols = centered_key_columns.astype(jnp.bfloat16)
    left = jnp.dot(ln_rows, first_factor_matrix, preferred_element_type=jnp.float32).astype(jnp.bfloat16)
    right = jnp.dot(ln_cols, second_factor_matrix, preferred_element_type=jnp.float32).astype(jnp.bfloat16)
    right_wide = right.astype(jnp.float32)
    block = 8
    count = SOURCE_POSITIONS // block
    averaging_factor = 1.0 / HOMOLOG_TOTAL

    def step(carry, index):
        acc_right, acc_out, acc_bias = carry
        start = (index * block).astype(jnp.int32)
        left_blk = lax.dynamic_slice_in_dim(left, start, block, 1).astype(jnp.float32)
        grad_blk = lax.dynamic_slice_in_dim(pair_cotangent, start, block, 0)
        outer = (jnp.einsum('sic,sje->ijce', left_blk, right_wide) * averaging_factor).astype(jnp.bfloat16)
        outer = outer.reshape(block * TARGET_POSITIONS, PROJECTED_WIDTH * PROJECTED_WIDTH)
        pair = (jnp.dot(outer, output_weight, preferred_element_type=jnp.float32) + output_bias).astype(jnp.bfloat16)
        grad_flat = grad_blk.reshape(block * TARGET_POSITIONS, ZPLANE_FEATURES)
        d_outer = jnp.dot(grad_flat, output_weight.T, preferred_element_type=jnp.float32).astype(jnp.bfloat16)
        d_outer = d_outer.reshape(block, TARGET_POSITIONS, PROJECTED_WIDTH, PROJECTED_WIDTH).astype(jnp.float32)
        d_left_blk = jnp.einsum('ijce,sje->sic', d_outer, right_wide) * averaging_factor
        acc_right = acc_right + jnp.einsum('ijce,sic->sje', d_outer, left_blk) * averaging_factor
        acc_out = acc_out + jnp.dot(outer.T, grad_flat, preferred_element_type=jnp.float32)
        acc_bias = acc_bias + lax.optimization_barrier(jnp.sum(grad_flat.astype(jnp.float32), axis=0))
        return ((acc_right, acc_out, acc_bias), (pair.reshape(block, TARGET_POSITIONS, ZPLANE_FEATURES), d_left_blk))
    starting_state = (jnp.zeros((HOMOLOG_TOTAL, TARGET_POSITIONS, PROJECTED_WIDTH), jnp.float32), jnp.zeros((PROJECTED_WIDTH * PROJECTED_WIDTH, ZPLANE_FEATURES), jnp.float32), jnp.zeros((ZPLANE_FEATURES,), jnp.float32))
    (sum_right, grad_w_out, grad_b_out), (pairs, first_factor_vectors) = lax.scan(step, starting_state, jnp.arange(count, dtype=jnp.int32))
    pair_update = pairs.reshape(SOURCE_POSITIONS, TARGET_POSITIONS, ZPLANE_FEATURES)
    first_factor_gradient = jnp.transpose(first_factor_vectors, (1, 0, 2, 3)).reshape(HOMOLOG_TOTAL, SOURCE_POSITIONS, PROJECTED_WIDTH).astype(jnp.bfloat16)
    d_right = sum_right.astype(jnp.bfloat16)
    grad_w_left = jnp.einsum('sim,sic->mc', ln_rows.astype(jnp.float32), first_factor_gradient.astype(jnp.float32))
    grad_w_right = jnp.einsum('sim,sic->mc', ln_cols.astype(jnp.float32), d_right.astype(jnp.float32))
    back_rows = jnp.dot(first_factor_gradient, first_factor_matrix.T, preferred_element_type=jnp.float32)
    back_cols = jnp.dot(d_right, second_factor_matrix.T, preferred_element_type=jnp.float32)
    grad_rows = norm_back(back_rows, centered_query_rows, inverse_std_rows)
    grad_cols = norm_back(back_cols, centered_key_columns, inverse_std_columns)
    return (pair_update, grad_rows, grad_cols, grad_w_out, grad_b_out, grad_w_left, grad_w_right)
```

```python
import jax
import jax.numpy as jnp
from jax import lax
from jax.experimental import pallas as pl
from jax.experimental.pallas import tpu as pltpu
from jax.sharding import PartitionSpec as P

F32, BF16 = jnp.float32, jnp.bfloat16
MESH = pl.DeviceIdType.MESH
EPS = 1e-05

NQ, NK, NZ, NXY = 8, 32, 8, 16


def nn(a, b):
    return jnp.dot(a, b, preferred_element_type=F32)


def nt(a, b):
    return lax.dot_general(a, b, (((1,), (1,)), ((), ())), preferred_element_type=F32)


def mean_of(v):
    return jnp.mean(v, axis=-1, keepdims=True)


def normalize(v):
    center = v - mean_of(v)
    inv = lax.rsqrt(mean_of(center * center) + EPS)
    return center * inv, inv


def norm_back(g, hat, inv):
    return inv * (g - mean_of(g) - hat * mean_of(g * hat))


def iota(shape, dim):
    return lax.broadcasted_iota(jnp.int32, shape, dim)


def loop(lo, hi, body):
    def step(d, carry):
        body(d)
        return carry

    lax.fori_loop(lo, hi, step, 0)


def kernel(
    xs_ref, xc_ref, w1_ref, w2_ref, w_ref, b_ref, g_hbm,
    pair_hbm, grows_ref, gcols_ref, gw_ref, gb_ref, gwl_ref, gwr_ref,
    g, gs, pf, po, w4, w2t, xsf, hat_r, hat_c, inv_r, inv_c,
    rf, rm, rl, ap, bp, lf, lmf, lm, lt, dlf, dsf, drf, gwp,
    rbuf, lbuf, sdl, rdl, sdr, rdr,
    bsend, bcore, bxy, bz,
    sgc, rgc, sgx, rgx, rgz, fgw,
    sm, ssm, rsc, rsx, rsz, fsm,
    lsem, ssem, rsem,
):
    me_q, me_k = lax.axis_index("qrow"), lax.axis_index("kcol")
    me_z = lax.div(me_k, 4)
    me_x = lax.rem(lax.div(me_k, 2), 2)
    core = lax.rem(me_k, 2)
    me_p = me_x * 8 + me_q

    def at_k(d):
        k = lax.rem(me_k + d, NK)
        return k, (me_q, k)

    def at_q(d):
        q = lax.rem(me_q + d, NQ)
        return q, (q, me_k)

    def at_p(d):
        p = lax.rem(me_p + d, NXY)
        return p, (lax.rem(p, 8), me_z * 4 + lax.div(p, 8) * 2 + core)

    def at_z(d):
        z = lax.rem(me_z + d, NZ)
        return z, (me_q, z * 4 + me_x * 2 + core)

    mate = (me_q, me_k + 1 - 2 * core)

    def send(src, dst, n, device):
        pltpu.make_async_remote_copy(
            src_ref=src, dst_ref=dst, send_sem=ssem.at[n], recv_sem=rsem.at[n],
            device_id=device, device_id_type=MESH,
        ).start()

    def arrived(ref, n):
        pltpu.make_async_copy(ref, ref, rsem.at[n]).wait()

    def sent(ref, n):
        pltpu.make_async_copy(ref, ref, ssem.at[n]).wait()

    load_g = pltpu.make_async_copy(g_hbm, g, lsem.at[0])
    load_g.start()

    barrier = pltpu.get_barrier_semaphore()

    def greet(device):
        pl.semaphore_signal(barrier, inc=1, device_id=device, device_id_type=MESH)

    loop(1, NK, lambda d: greet(at_k(d)[1]))
    loop(1, NQ, lambda d: greet(at_q(d)[1]))
    loop(1, NQ, lambda d: greet((at_q(d)[0], me_z * 4 + (1 - me_x) * 2 + core)))

    lane_group = lax.shift_right_logical(iota((16, 128), 1), 5)
    lane_s = jnp.bitwise_and(iota((16, 512), 1), 15) == iota((16, 512), 0)
    fold = (lax.shift_right_logical(iota((128, 512), 1), 4) == iota((128, 512), 0)).astype(BF16)

    spread = (jnp.bitwise_and(iota((32, 128), 1), 31) == iota((32, 128), 0)).astype(BF16)
    w2t[...] = nn(w2_ref[...], spread).astype(BF16)
    hat, inv = normalize(xc_ref[...].astype(F32).reshape(128, 256))
    hat_c[...] = hat
    inv_c[...] = jnp.broadcast_to(inv, (128, 128))
    right = nn(hat.astype(BF16), w2t[...]).astype(BF16).astype(F32)
    tiles = []
    for t in range(2):
        tile = right[t * 64 : t * 64 + 16, :]
        for jg in range(1, 4):
            tile = jnp.where(lane_group == jg, right[t * 64 + jg * 16 : t * 64 + jg * 16 + 16, :], tile)
        tiles.append(tile)
    rbuf[me_q] = jnp.concatenate(tiles, axis=0).astype(BF16)

    for h in range(2):
        for s in range(16):
            xsf[h, s * 8 : s * 8 + 3, :] = xs_ref[s, :, h * 128 : (h + 1) * 128].astype(F32)
    rows = jnp.concatenate(
        [
            jnp.concatenate([xsf[h, pl.ds(i3, 16, stride=8), :] for h in range(2)], axis=1)
            for i3 in range(3)
        ],
        axis=0,
    )
    hat, inv = normalize(rows)
    hat_r[...] = hat
    inv_r[...] = jnp.broadcast_to(inv, (48, 128))
    left = nn(hat.astype(BF16), w1_ref[...]).astype(BF16)
    tile = jnp.zeros((16, 128), F32)
    for i3 in range(3):
        wide = nn(left[i3 * 16 : i3 * 16 + 16, :], fold[0:32, :])
        row = jnp.sum(jnp.where(lane_s, wide, 0.0), axis=0, keepdims=True)
        for cq in range(4):
            piece = jnp.broadcast_to(row[:, cq * 128 : (cq + 1) * 128], (16, 128))
            tile = jnp.where(iota((16, 128), 0) == i3 * 4 + cq, piece, tile)
    lbuf[me_k] = tile.astype(BF16)

    for c in range(32):
        block = w_ref[c * 32 : (c + 1) * 32, :]
        for jg in range(4):
            w4[jg * 32 : (jg + 1) * 32, c * 128 : (c + 1) * 128] = block

    load_g.wait()

    def widen(n, total):
        for u in range(4):
            v = g[4 * n + u].astype(F32)
            pf[pl.ds(pl.multiple_of((4 * n + u) * 64, 64), 64), :] = v
            total = total + v
        return total

    total = lax.fori_loop(0, 24, widen, jnp.zeros((64, 128), F32))
    bsend[...] = jnp.broadcast_to(jnp.sum(total, axis=0, keepdims=True), (8, 128))

    def turn(n):
        for u in range(4):
            lanes = pl.ds(pl.multiple_of((4 * n + u) * 128, 128), 128)
            gs[:, lanes] = pf[pl.ds(4 * n + u, 96, stride=64), :].astype(BF16)

    loop(0, 16, turn)

    pl.semaphore_wait(barrier, NK + 2 * NQ - 3)

    loop(1, NQ, lambda d: send(rbuf.at[me_q], rbuf.at[me_q], 0, at_q(d)[1]))
    loop(1, NK, lambda d: send(lbuf.at[me_k], lbuf.at[me_k], 1, at_k(d)[1]))
    send(bsend, bcore, 2, mate)

    arrived(rbuf.at[pl.ds(0, NQ - 1)], 0)
    for s in range(16):
        part = rbuf[s // 2, (s % 2) * 16 : (s % 2) * 16 + 16, :].astype(F32)
        rf[pl.ds(s, 16, stride=16), :] = part * (1.0 / 16.0)
    rx = rf[...]
    group = lax.shift_right_logical(iota((256, 128), 1), 5)
    for jg in range(4):
        rm[jg * 256 : (jg + 1) * 256, :] = jnp.where(group == jg, rx, 0.0).astype(BF16)
    rxt = rx.T
    for jg in range(4):
        rl[:, jg * 256 : (jg + 1) * 256] = rxt[jg * 32 : (jg + 1) * 32, :].astype(BF16)

    def make_a(jg):
        for cc in range(16):
            r = nn(
                rm[pl.ds(pl.multiple_of(jg * 256, 256), 256), :],
                w4[:, cc * 256 : (cc + 1) * 256],
            ).astype(BF16)
            for j in range(16):
                lanes = pl.ds(pl.multiple_of((jg * 16 + j) * 128, 128), 128)
                for h in range(2):
                    to = cc * 32 + h * 16
                    ap[to : to + 16, lanes] = r[j * 16 : (j + 1) * 16, h * 128 : (h + 1) * 128]

    loop(0, 4, make_a)

    dl = nt(gs[:, 0:4096], ap[:, 0:4096]) + nt(gs[:, 4096:8192], ap[:, 4096:8192])
    for cq in range(4):
        dlf[cq] = dl[:, cq * 128 : (cq + 1) * 128]
    dsf[...] = jnp.zeros((512, 128), F32)
    for i3 in range(3):
        for cq in range(4):
            dsf[pl.ds(i3 * 4 + cq, 32, stride=16), :] = dlf[cq, pl.ds(i3, 32, stride=3), :]
    sdl[...] = dsf[...].astype(BF16).reshape(32, 16, 128)
    rdl[me_k] = sdl[me_k]

    def send_dl(d):
        k, device = at_k(d)
        send(sdl.at[k], rdl.at[me_k], 3, device)

    loop(1, NK, send_dl)

    arrived(lbuf.at[pl.ds(0, NK - 1)], 1)
    lf[...] = lbuf[...].astype(F32).reshape(512, 128)
    for cq in range(4):
        for i3 in range(3):
            lmf[cq, pl.ds(i3, 32, stride=3), :] = lf[pl.ds(i3 * 4 + cq, 32, stride=16), :]
    for cq in range(4):
        lm[:, cq * 128 : (cq + 1) * 128] = lmf[cq].astype(BF16)
        lt[cq * 128 : (cq + 1) * 128, :] = lmf[cq].T.astype(BF16)

    arrived(bcore, 2)
    bxy[me_p] = bsend[...] + bcore[...]
    loop(1, NXY, lambda d: send(bxy.at[me_p], bxy.at[me_p], 4, at_p(d)[1]))

    def make_b(jg):
        for p in range(8):
            lanes = pl.ds(pl.multiple_of(jg * 2048 + p * 256, 256), 256)
            r = nn(lt[...], gs[:, lanes]).astype(BF16)
            for c in range(32):
                for h in range(2):
                    to = (p * 2 + h) * 16
                    bp[jg, to : to + 16, c * 128 : (c + 1) * 128] = r[c * 16 : (c + 1) * 16, h * 128 : (h + 1) * 128]

    loop(0, 4, make_b)

    dr = jnp.zeros((256, 128), F32)
    for jg in range(4):
        dr = dr + jnp.where(group == jg, nt(bp[jg], w4[...]), 0.0)
    drf[...] = dr * (1.0 / 16.0)
    for s in range(16):
        sdr[s // 2, (s % 2) * 16 : (s % 2) * 16 + 16, :] = drf[pl.ds(s, 16, stride=16), :].astype(BF16)
    rdr[me_q] = sdr[me_q]

    def send_dr(d):
        q, device = at_q(d)
        send(sdr.at[q], rdr.at[me_q], 5, device)

    loop(1, NQ, send_dr)

    for n in range(4):
        lanes = slice(n * 1024, (n + 1) * 1024)
        r = nn(rl[:, 0:256], bp[0, :, lanes])
        for jg in range(1, 4):
            r = r + nn(rl[:, jg * 256 : (jg + 1) * 256], bp[jg, :, lanes])
        gwp[:, lanes] = r
    sgc[...] = gwp[:, pl.ds(pl.multiple_of((1 - core) * 2048, 2048), 2048)].astype(BF16)
    send(sgc, rgc, 6, mate)

    def make_p(jg):
        for p in range(8):
            lanes = pl.ds(pl.multiple_of(jg * 2048 + p * 256, 256), 256)
            r = nn(lm[...], ap[:, lanes])
            for h in range(2):
                pf[pl.ds(jg * 16 + 2 * p + h, 96, stride=64), :] = r[:, h * 128 : (h + 1) * 128]

    loop(0, 2, make_p)

    arrived(rgc, 6)
    for p in range(16):
        lanes = pl.ds(pl.multiple_of(core * 2048 + p * 128, 128), 128)
        half = gwp[:, lanes] + rgc[:, p * 128 : (p + 1) * 128].astype(F32)
        sgx[p] = half.astype(BF16)
    rgx[me_p] = sgx[me_p]

    def send_gx(d):
        p, device = at_p(d)
        send(sgx.at[p], rgx.at[me_p], 7, device)

    loop(1, NXY, send_gx)

    arrived(rdl.at[pl.ds(0, NK - 1)], 3)
    dsum = rdl[0].astype(F32)
    for k in range(1, NK):
        dsum = dsum + rdl[k].astype(F32)
    dsum = dsum.astype(BF16).astype(F32)
    parts = []
    for i3 in range(3):
        row = jnp.concatenate([dsum[i3 * 4 + cq : i3 * 4 + cq + 1, :] for cq in range(4)], axis=1)
        parts.append(jnp.where(lane_s, jnp.broadcast_to(row, (16, 512)), 0.0))
    dleft = nt(jnp.concatenate(parts, axis=0).astype(BF16), fold)
    hat = hat_r[...]
    sm[0] = nn(dleft.T[0:32, :].astype(BF16), hat.astype(BF16))
    back = nt(dleft[:, 0:32].astype(BF16), w1_ref[...])
    out = norm_back(back, hat, inv_r[:, 0:1])
    for h in range(2):
        for i3 in range(3):
            xsf[h, pl.ds(i3, 16, stride=8), :] = out[i3 * 16 : i3 * 16 + 16, h * 128 : (h + 1) * 128]
        for s in range(16):
            grows_ref[s, :, h * 128 : (h + 1) * 128] = xsf[h, s * 8 : s * 8 + 3, :].astype(BF16)

    arrived(bxy.at[pl.ds(0, NXY - 1)], 4)
    total = bxy[0]
    for p in range(1, NXY):
        total = total + bxy[p]
    bz[me_z] = total
    loop(1, NZ, lambda d: send(bz.at[me_z], bz.at[me_z], 8, at_z(d)[1]))

    arrived(rdr.at[pl.ds(0, NQ - 1)], 5)
    dsum = rdr[0].astype(F32)
    for q in range(1, NQ):
        dsum = dsum + rdr[q].astype(F32)
    dsum = dsum.astype(BF16).astype(F32)
    parts = []
    for t in range(2):
        for jg in range(4):
            parts.append(jnp.where(lane_group == jg, dsum[t * 16 : t * 16 + 16, :], 0.0))
    dright = jnp.concatenate(parts, axis=0)
    hat = hat_c[...]
    term = nn(dright.T.astype(BF16), hat.astype(BF16))
    sm[1] = term[0:32, :] + term[32:64, :] + term[64:96, :] + term[96:128, :]
    ssm[...] = sm[1 - core].astype(BF16)
    send(ssm, rsc, 9, mate)
    back = nt(dright.astype(BF16), w2t[...])
    out = norm_back(back, hat, inv_c[:, 0:1])
    gcols_ref[...] = out.reshape(2, 64, 256).astype(BF16)

    arrived(rsc, 9)
    rsx[me_p] = (sm[core] + rsc[...].astype(F32)).astype(BF16)
    loop(1, NXY, lambda d: send(rsx.at[me_p], rsx.at[me_p], 10, at_p(d)[1]))

    arrived(rgx.at[pl.ds(0, NXY - 1)], 7)
    total = rgx[0].astype(F32)
    for p in range(1, NXY):
        total = total + rgx[p].astype(F32)
    rgz[me_z] = total.astype(BF16)
    loop(1, NZ, lambda d: send(rgz.at[me_z], rgz.at[me_z], 11, at_z(d)[1]))

    loop(2, 4, make_p)
    bias = b_ref[...]

    def finish(n):
        for u in range(4):
            rows = pf[pl.ds(pl.multiple_of((4 * n + u) * 64, 64), 64), :]
            po[4 * n + u] = (rows + bias).astype(BF16)

    loop(0, 24, finish)
    store_pair = pltpu.make_async_copy(po, pair_hbm, lsem.at[1])
    store_pair.start()

    arrived(rsx.at[pl.ds(0, NXY - 1)], 10)
    total = rsx[0].astype(F32)
    for p in range(1, NXY):
        total = total + rsx[p].astype(F32)
    rsz[me_z] = total.astype(BF16)
    loop(1, NZ, lambda d: send(rsz.at[me_z], rsz.at[me_z], 12, at_z(d)[1]))

    arrived(rgz.at[pl.ds(0, NZ - 1)], 11)
    total = rgz[0].astype(F32)
    for z in range(1, NZ):
        total = total + rgz[z].astype(F32)
    fgw[core, me_p] = total.astype(BF16)
    loop(1, NXY, lambda d: send(fgw.at[core, me_p], fgw.at[core, me_p], 13, at_p(d)[1]))

    arrived(bz.at[pl.ds(0, NZ - 1)], 8)
    total = bz[0]
    for z in range(1, NZ):
        total = total + bz[z]
    gb_ref[...] = total[0:1, :]

    arrived(rsz.at[pl.ds(0, NZ - 1)], 12)
    total = rsz[0].astype(F32)
    for z in range(1, NZ):
        total = total + rsz[z].astype(F32)
    fsm[core] = total
    send(fsm.at[core], fsm.at[core], 14, mate)
    arrived(fsm.at[0], 14)
    gwl_ref[...] = fsm[0].T
    gwr_ref[...] = fsm[1].T

    arrived(fgw.at[0, pl.ds(0, NXY - 1)], 13)
    send(fgw.at[core], fgw.at[core], 15, mate)
    mine = pl.ds(pl.multiple_of(core * 512, 512), 512)
    gw_ref[mine, :] = fgw[core].astype(F32).reshape(512, 128)
    arrived(fgw.at[0], 15)
    other = pl.ds(pl.multiple_of((1 - core) * 512, 512), 512)
    gw_ref[other, :] = fgw[1 - core].astype(F32).reshape(512, 128)

    store_pair.wait()
    sent(rbuf.at[pl.ds(0, NQ - 1)], 0)
    sent(lbuf.at[pl.ds(0, NK - 1)], 1)
    sent(bsend, 2)
    sent(rdl.at[pl.ds(0, NK - 1)], 3)
    sent(bxy.at[pl.ds(0, NXY - 1)], 4)
    sent(rdr.at[pl.ds(0, NQ - 1)], 5)
    sent(rgc, 6)
    sent(rgx.at[pl.ds(0, NXY - 1)], 7)
    sent(bz.at[pl.ds(0, NZ - 1)], 8)
    sent(ssm, 9)
    sent(rsx.at[pl.ds(0, NXY - 1)], 10)
    sent(rgz.at[pl.ds(0, NZ - 1)], 11)
    sent(rsz.at[pl.ds(0, NZ - 1)], 12)
    sent(fgw.at[0, pl.ds(0, NXY - 1)], 13)
    sent(fsm.at[0], 14)
    sent(fgw.at[0], 15)


SCRATCH = (
    ((96, 64, 128), BF16),
    ((96, 8192), BF16),
    ((6144, 128), F32),
    ((96, 64, 128), BF16),
    ((128, 4096), BF16),
    ((256, 128), BF16),
    ((2, 128, 128), F32),
    ((48, 256), F32),
    ((128, 256), F32),
    ((48, 128), F32),
    ((128, 128), F32),
    ((256, 128), F32),
    ((1024, 128), BF16),
    ((32, 1024), BF16),
    ((512, 8192), BF16),
    ((4, 256, 4096), BF16),
    ((512, 128), F32),
    ((4, 96, 128), F32),
    ((96, 512), BF16),
    ((512, 96), BF16),
    ((4, 96, 128), F32),
    ((512, 128), F32),
    ((256, 128), F32),
    ((32, 4096), F32),
    ((NQ, 32, 128), BF16),
    ((NK, 16, 128), BF16),
    ((NK, 16, 128), BF16),
    ((NK, 16, 128), BF16),
    ((NQ, 32, 128), BF16),
    ((NQ, 32, 128), BF16),
    ((8, 128), F32),
    ((8, 128), F32),
    ((NXY, 8, 128), F32),
    ((NZ, 8, 128), F32),
    ((32, 2048), BF16),
    ((32, 2048), BF16),
    ((NXY, 32, 128), BF16),
    ((NXY, 32, 128), BF16),
    ((NZ, 32, 128), BF16),
    ((2, NXY, 32, 128), BF16),
    ((2, 32, 256), F32),
    ((32, 256), BF16),
    ((32, 256), BF16),
    ((NXY, 32, 256), BF16),
    ((NZ, 32, 256), BF16),
    ((2, 32, 256), F32),
)
SENDS = 16


def local(xs, xc, w1, w2, w, b, g):
    vmem = pl.BlockSpec(memory_space=pltpu.VMEM)
    hbm = pl.BlockSpec(memory_space=pl.ANY)
    pair, grows, gcols, gw, gb, gwl, gwr = pl.pallas_call(
        kernel,
        out_shape=(
            jax.ShapeDtypeStruct((96, 64, 128), BF16),
            jax.ShapeDtypeStruct((16, 3, 256), BF16),
            jax.ShapeDtypeStruct((2, 64, 256), BF16),
            jax.ShapeDtypeStruct((1024, 128), F32),
            jax.ShapeDtypeStruct((1, 128), F32),
            jax.ShapeDtypeStruct((256, 32), F32),
            jax.ShapeDtypeStruct((256, 32), F32),
        ),
        in_specs=[vmem] * 6 + [hbm],
        out_specs=(hbm,) + (vmem,) * 6,
        scratch_shapes=[pltpu.VMEM(shape, dtype) for shape, dtype in SCRATCH]
        + [pltpu.SemaphoreType.DMA((2,))]
        + [pltpu.SemaphoreType.DMA((SENDS,))] * 2,
        compiler_params=pltpu.CompilerParams(
            collective_id=0, has_side_effects=True, vmem_limit_bytes=56 << 20
        ),
        cost_estimate=pl.CostEstimate(flops=3_300_000_000, bytes_accessed=5_000_000, transcendentals=0),
    )(xs, xc, w1, w2, w, b.reshape(1, 128), g)
    return pair, grows, gcols, gw, gb.reshape(128), gwl, gwr


def solution(mesh):
    return jax.shard_map(
        local,
        mesh=mesh,
        in_specs=(
            P(None, ("qrow", "kcol"), None),
            P("qrow", "kcol", None),
            P(),
            P(),
            P(),
            P(),
            P("qrow", "kcol", None),
        ),
        out_specs=(
            P("qrow", "kcol", None),
            P(None, ("qrow", "kcol"), None),
            P("qrow", "kcol", None),
            P(),
            P(),
            P(),
            P(),
        ),
        check_vma=False,
    )
```

```python
import jax
import jax.numpy as jnp
from jax import lax
from jax.experimental import pallas as pl
from jax.experimental.pallas import tpu as pltpu
from jax.sharding import PartitionSpec as P

F32, BF16 = jnp.float32, jnp.bfloat16
MESH = pl.DeviceIdType.MESH
EPS = 1e-05

NQ, NK, NZ, NXY = 8, 32, 8, 16


def nn(a, b):
    return jnp.dot(a, b, preferred_element_type=F32)


def nt(a, b):
    return lax.dot_general(a, b, (((1,), (1,)), ((), ())), preferred_element_type=F32)


def mean_of(v):
    return jnp.mean(v, axis=-1, keepdims=True)


def normalize(v):
    center = v - mean_of(v)
    inv = lax.rsqrt(mean_of(center * center) + EPS)
    return center * inv, inv


def norm_back(g, hat, inv):
    return inv * (g - mean_of(g) - hat * mean_of(g * hat))


def iota(shape, dim):
    return lax.broadcasted_iota(jnp.int32, shape, dim)


def loop(lo, hi, body):
    def step(d, carry):
        body(d)
        return carry

    lax.fori_loop(lo, hi, step, 0)


def kernel(
    xs_hbm, xc_hbm, w1_hbm, w2_hbm, w_hbm, b_hbm, g_hbm,
    pair_hbm, grows_hbm, gcols_hbm, gw_hbm, gb_hbm, gwl_hbm, gwr_hbm,
    xs_ref, xc_ref, w1_ref, w2_ref, w_ref, b_ref, grows_ref, gcols_ref, gw_ref, gb_ref,
    g, gs, pf, po, w4, w2r, hat_r, hat_c, inv_r, inv_c,
    rf, rm, rl, ap, bp, lf, lmf, lm, lt, dlf, dsf, drf, gwp,
    rbuf, lbuf, sdl, rdl, sdr, rdr,
    bsend, bcore, bxy, bz,
    sgc, rgc, sgx, rgx, rgz, fgw,
    sm, ssm, rsc, rsx, rsz, fsm,
    lsem, ssem, rsem,
):
    me_q, me_k = lax.axis_index("qrow"), lax.axis_index("kcol")
    me_z = lax.div(me_k, 4)
    me_x = lax.rem(lax.div(me_k, 2), 2)
    core = lax.rem(me_k, 2)
    me_p = me_x * 8 + me_q

    def at_k(d):
        k = lax.rem(me_k + d, NK)
        return k, (me_q, k)

    def at_q(d):
        q = lax.rem(me_q + d, NQ)
        return q, (q, me_k)

    def at_p(d):
        p = lax.rem(me_p + d, NXY)
        return p, (lax.rem(p, 8), me_z * 4 + lax.div(p, 8) * 2 + core)

    def at_z(d):
        z = lax.rem(me_z + d, NZ)
        return z, (me_q, z * 4 + me_x * 2 + core)

    mate = (me_q, me_k + 1 - 2 * core)

    def send(src, dst, n, device):
        pltpu.make_async_remote_copy(
            src_ref=src, dst_ref=dst, send_sem=ssem.at[n], recv_sem=rsem.at[n],
            device_id=device, device_id_type=MESH,
        ).start()

    def arrived(ref, n):
        pltpu.make_async_copy(ref, ref, rsem.at[n]).wait()

    def sent(ref, n):
        pltpu.make_async_copy(ref, ref, ssem.at[n]).wait()

    def fetch(src, dst, n):
        copy = pltpu.make_async_copy(src, dst, lsem.at[n])
        copy.start()
        return copy

    load_xc = fetch(xc_hbm, xc_ref, 0)
    load_w2 = fetch(w2_hbm, w2_ref, 1)
    load_xs = fetch(xs_hbm, xs_ref, 2)
    load_w1 = fetch(w1_hbm, w1_ref, 3)
    load_g = fetch(g_hbm, g, 4)
    load_w = fetch(w_hbm, w_ref, 5)
    load_b = fetch(b_hbm, b_ref, 6)

    barrier = pltpu.get_barrier_semaphore()

    def greet(device):
        pl.semaphore_signal(barrier, inc=1, device_id=device, device_id_type=MESH)

    loop(1, NK, lambda d: greet(at_k(d)[1]))
    loop(1, NQ, lambda d: greet(at_q(d)[1]))
    loop(1, NQ, lambda d: greet((at_q(d)[0], me_z * 4 + (1 - me_x) * 2 + core)))

    lane_group = lax.shift_right_logical(iota((16, 128), 1), 5)
    lane_s = jnp.bitwise_and(iota((16, 512), 1), 15) == iota((16, 512), 0)
    fold = (lax.shift_right_logical(iota((128, 512), 1), 4) == iota((128, 512), 0)).astype(BF16)

    load_xc.wait()
    load_w2.wait()
    for jg in range(4):
        w2r[jg * 32 : (jg + 1) * 32, :] = w2_ref[...]
    hat, inv = normalize(xc_ref[...].astype(F32).reshape(128, 256))
    hat_c[...] = hat
    inv_c[...] = jnp.broadcast_to(inv, (128, 128))
    right = nt(hat.astype(BF16), w2r[...]).astype(BF16).astype(F32)
    tiles = []
    for t in range(2):
        tile = right[t * 64 : t * 64 + 16, :]
        for jg in range(1, 4):
            tile = jnp.where(lane_group == jg, right[t * 64 + jg * 16 : t * 64 + jg * 16 + 16, :], tile)
        tiles.append(tile)
    rbuf[me_q] = jnp.concatenate(tiles, axis=0).astype(BF16)

    load_xs.wait()
    load_w1.wait()
    hat, inv = normalize(xs_ref[...].astype(F32).reshape(48, 256))
    hat_r[...] = hat
    inv_r[...] = jnp.broadcast_to(inv, (48, 128))
    left = nt(hat.astype(BF16), w1_ref[...]).astype(BF16)
    tile = jnp.zeros((16, 128), F32)
    for i3 in range(3):
        wide = nn(left[i3 * 16 : i3 * 16 + 16, :], fold[0:32, :])
        row = jnp.sum(jnp.where(lane_s, wide, 0.0), axis=0, keepdims=True)
        for cq in range(4):
            piece = jnp.broadcast_to(row[:, cq * 128 : (cq + 1) * 128], (16, 128))
            tile = jnp.where(iota((16, 128), 0) == i3 * 4 + cq, piece, tile)
    lbuf[me_k] = tile.astype(BF16)

    load_w.wait()
    for c in range(32):
        block = w_ref[c * 32 : (c + 1) * 32, :]
        for jg in range(4):
            w4[jg * 32 : (jg + 1) * 32, c * 128 : (c + 1) * 128] = block

    load_g.wait()

    def widen(n, total):
        for u in range(4):
            v = g[4 * n + u].astype(F32)
            pf[pl.ds(pl.multiple_of((4 * n + u) * 64, 64), 64), :] = v
            total = total + v
        return total

    total = lax.fori_loop(0, 24, widen, jnp.zeros((64, 128), F32))
    bsend[...] = jnp.broadcast_to(jnp.sum(total, axis=0, keepdims=True), (8, 128))

    def turn(n):
        for u in range(4):
            lanes = pl.ds(pl.multiple_of((4 * n + u) * 128, 128), 128)
            gs[:, lanes] = pf[pl.ds(4 * n + u, 96, stride=64), :].astype(BF16)

    loop(0, 16, turn)

    pl.semaphore_wait(barrier, NK + 2 * NQ - 3)

    loop(1, NQ, lambda d: send(rbuf.at[me_q], rbuf.at[me_q], 0, at_q(d)[1]))
    loop(1, NK, lambda d: send(lbuf.at[me_k], lbuf.at[me_k], 1, at_k(d)[1]))
    send(bsend, bcore, 2, mate)

    arrived(rbuf.at[pl.ds(0, NQ - 1)], 0)
    for s in range(16):
        part = rbuf[s // 2, (s % 2) * 16 : (s % 2) * 16 + 16, :].astype(F32)
        rf[pl.ds(s, 16, stride=16), :] = part * (1.0 / 16.0)
    rx = rf[...]
    group = lax.shift_right_logical(iota((256, 128), 1), 5)
    for jg in range(4):
        rm[jg * 256 : (jg + 1) * 256, :] = jnp.where(group == jg, rx, 0.0).astype(BF16)
    rxt = rx.T
    for jg in range(4):
        rl[:, jg * 256 : (jg + 1) * 256] = rxt[jg * 32 : (jg + 1) * 32, :].astype(BF16)

    def make_a(jg):
        for cc in range(16):
            r = nn(
                rm[pl.ds(pl.multiple_of(jg * 256, 256), 256), :],
                w4[:, cc * 256 : (cc + 1) * 256],
            ).astype(BF16)
            for j in range(16):
                lanes = pl.ds(pl.multiple_of((jg * 16 + j) * 128, 128), 128)
                for h in range(2):
                    to = cc * 32 + h * 16
                    ap[to : to + 16, lanes] = r[j * 16 : (j + 1) * 16, h * 128 : (h + 1) * 128]

    loop(0, 4, make_a)

    dl = nt(gs[:, 0:4096], ap[:, 0:4096]) + nt(gs[:, 4096:8192], ap[:, 4096:8192])
    for cq in range(4):
        dlf[cq] = dl[:, cq * 128 : (cq + 1) * 128]
    dsf[...] = jnp.zeros((512, 128), F32)
    for i3 in range(3):
        for cq in range(4):
            dsf[pl.ds(i3 * 4 + cq, 32, stride=16), :] = dlf[cq, pl.ds(i3, 32, stride=3), :]
    sdl[...] = dsf[...].astype(BF16).reshape(32, 16, 128)
    rdl[me_k] = sdl[me_k]

    def send_dl(d):
        k, device = at_k(d)
        send(sdl.at[k], rdl.at[me_k], 3, device)

    loop(1, NK, send_dl)

    arrived(lbuf.at[pl.ds(0, NK - 1)], 1)
    lf[...] = lbuf[...].astype(F32).reshape(512, 128)
    for cq in range(4):
        for i3 in range(3):
            lmf[cq, pl.ds(i3, 32, stride=3), :] = lf[pl.ds(i3 * 4 + cq, 32, stride=16), :]
    for cq in range(4):
        lm[:, cq * 128 : (cq + 1) * 128] = lmf[cq].astype(BF16)
        lt[cq * 128 : (cq + 1) * 128, :] = lmf[cq].T.astype(BF16)

    arrived(bcore, 2)
    bxy[me_p] = bsend[...] + bcore[...]
    loop(1, NXY, lambda d: send(bxy.at[me_p], bxy.at[me_p], 4, at_p(d)[1]))

    def make_b(jg):
        for p in range(8):
            lanes = pl.ds(pl.multiple_of(jg * 2048 + p * 256, 256), 256)
            r = nn(lt[...], gs[:, lanes]).astype(BF16)
            for c in range(32):
                for h in range(2):
                    to = (p * 2 + h) * 16
                    bp[jg, to : to + 16, c * 128 : (c + 1) * 128] = r[c * 16 : (c + 1) * 16, h * 128 : (h + 1) * 128]

    loop(0, 4, make_b)

    dr = jnp.zeros((256, 128), F32)
    for jg in range(4):
        dr = dr + jnp.where(group == jg, nt(bp[jg], w4[...]), 0.0)
    drf[...] = dr * (1.0 / 16.0)
    for s in range(16):
        sdr[s // 2, (s % 2) * 16 : (s % 2) * 16 + 16, :] = drf[pl.ds(s, 16, stride=16), :].astype(BF16)
    rdr[me_q] = sdr[me_q]

    def send_dr(d):
        q, device = at_q(d)
        send(sdr.at[q], rdr.at[me_q], 5, device)

    loop(1, NQ, send_dr)

    for n in range(4):
        lanes = slice(n * 1024, (n + 1) * 1024)
        r = nn(rl[:, 0:256], bp[0, :, lanes])
        for jg in range(1, 4):
            r = r + nn(rl[:, jg * 256 : (jg + 1) * 256], bp[jg, :, lanes])
        gwp[:, lanes] = r
    sgc[...] = gwp[:, pl.ds(pl.multiple_of((1 - core) * 2048, 2048), 2048)].astype(BF16)
    send(sgc, rgc, 6, mate)

    def make_p(jg):
        for p in range(8):
            lanes = pl.ds(pl.multiple_of(jg * 2048 + p * 256, 256), 256)
            r = nn(lm[...], ap[:, lanes])
            for h in range(2):
                pf[pl.ds(jg * 16 + 2 * p + h, 96, stride=64), :] = r[:, h * 128 : (h + 1) * 128]

    loop(0, 2, make_p)

    arrived(rgc, 6)
    for p in range(16):
        lanes = pl.ds(pl.multiple_of(core * 2048 + p * 128, 128), 128)
        half = gwp[:, lanes] + rgc[:, p * 128 : (p + 1) * 128].astype(F32)
        sgx[p] = half.astype(BF16)
    rgx[me_p] = sgx[me_p]

    def send_gx(d):
        p, device = at_p(d)
        send(sgx.at[p], rgx.at[me_p], 7, device)

    loop(1, NXY, send_gx)

    arrived(rdl.at[pl.ds(0, NK - 1)], 3)
    dsum = rdl[0].astype(F32)
    for k in range(1, NK):
        dsum = dsum + rdl[k].astype(F32)
    dsum = dsum.astype(BF16).astype(F32)
    parts = []
    for i3 in range(3):
        row = jnp.concatenate([dsum[i3 * 4 + cq : i3 * 4 + cq + 1, :] for cq in range(4)], axis=1)
        parts.append(jnp.where(lane_s, jnp.broadcast_to(row, (16, 512)), 0.0))
    dleft = nt(jnp.concatenate(parts, axis=0).astype(BF16), fold)
    hat = hat_r[...]
    sm[0] = nn(dleft.T[0:32, :].astype(BF16), hat.astype(BF16))
    back = nn(dleft[:, 0:32].astype(BF16), w1_ref[...])
    out = norm_back(back, hat, inv_r[:, 0:1])
    grows_ref[...] = out.reshape(3, 16, 256).astype(BF16)
    store_rows = fetch(grows_ref, grows_hbm, 7)

    arrived(bxy.at[pl.ds(0, NXY - 1)], 4)
    total = bxy[0]
    for p in range(1, NXY):
        total = total + bxy[p]
    bz[me_z] = total
    loop(1, NZ, lambda d: send(bz.at[me_z], bz.at[me_z], 8, at_z(d)[1]))

    arrived(rdr.at[pl.ds(0, NQ - 1)], 5)
    dsum = rdr[0].astype(F32)
    for q in range(1, NQ):
        dsum = dsum + rdr[q].astype(F32)
    dsum = dsum.astype(BF16).astype(F32)
    parts = []
    for t in range(2):
        for jg in range(4):
            parts.append(jnp.where(lane_group == jg, dsum[t * 16 : t * 16 + 16, :], 0.0))
    dright = jnp.concatenate(parts, axis=0)
    hat = hat_c[...]
    term = nn(dright.T.astype(BF16), hat.astype(BF16))
    sm[1] = term[0:32, :] + term[32:64, :] + term[64:96, :] + term[96:128, :]
    ssm[...] = sm[1 - core].astype(BF16)
    send(ssm, rsc, 9, mate)
    back = nn(dright.astype(BF16), w2r[...])
    out = norm_back(back, hat, inv_c[:, 0:1])
    gcols_ref[...] = out.reshape(2, 64, 256).astype(BF16)
    store_cols = fetch(gcols_ref, gcols_hbm, 8)

    arrived(rsc, 9)
    rsx[me_p] = (sm[core] + rsc[...].astype(F32)).astype(BF16)
    loop(1, NXY, lambda d: send(rsx.at[me_p], rsx.at[me_p], 10, at_p(d)[1]))

    arrived(rgx.at[pl.ds(0, NXY - 1)], 7)
    total = rgx[0].astype(F32)
    for p in range(1, NXY):
        total = total + rgx[p].astype(F32)
    rgz[me_z] = total.astype(BF16)
    loop(1, NZ, lambda d: send(rgz.at[me_z], rgz.at[me_z], 11, at_z(d)[1]))

    loop(2, 4, make_p)
    load_b.wait()
    bias = b_ref[...]

    def finish(n):
        for u in range(4):
            rows = pf[pl.ds(pl.multiple_of((4 * n + u) * 64, 64), 64), :]
            po[4 * n + u] = (rows + bias).astype(BF16)

    loop(0, 24, finish)
    store_pair = fetch(po, pair_hbm, 9)

    arrived(rsx.at[pl.ds(0, NXY - 1)], 10)
    total = rsx[0].astype(F32)
    for p in range(1, NXY):
        total = total + rsx[p].astype(F32)
    rsz[me_z] = total.astype(BF16)
    loop(1, NZ, lambda d: send(rsz.at[me_z], rsz.at[me_z], 12, at_z(d)[1]))

    arrived(rgz.at[pl.ds(0, NZ - 1)], 11)
    total = rgz[0].astype(F32)
    for z in range(1, NZ):
        total = total + rgz[z].astype(F32)
    fgw[core, me_p] = total.astype(BF16)
    loop(1, NXY, lambda d: send(fgw.at[core, me_p], fgw.at[core, me_p], 13, at_p(d)[1]))

    arrived(bz.at[pl.ds(0, NZ - 1)], 8)
    total = bz[0]
    for z in range(1, NZ):
        total = total + bz[z]
    gb_ref[...] = total[0:1, :]
    store_b = fetch(gb_ref, gb_hbm, 10)

    arrived(rsz.at[pl.ds(0, NZ - 1)], 12)
    total = rsz[0].astype(F32)
    for z in range(1, NZ):
        total = total + rsz[z].astype(F32)
    fsm[core] = total
    send(fsm.at[core], fsm.at[core], 14, mate)
    arrived(fsm.at[0], 14)
    store_wl = fetch(fsm.at[0], gwl_hbm, 11)
    store_wr = fetch(fsm.at[1], gwr_hbm, 12)

    arrived(fgw.at[0, pl.ds(0, NXY - 1)], 13)
    send(fgw.at[core], fgw.at[core], 15, mate)
    mine = pl.ds(pl.multiple_of(core * 512, 512), 512)
    gw_ref[mine, :] = fgw[core].astype(F32).reshape(512, 128)
    store_mine = fetch(gw_ref.at[mine], gw_hbm.at[mine], 13)
    arrived(fgw.at[0], 15)
    other = pl.ds(pl.multiple_of((1 - core) * 512, 512), 512)
    gw_ref[other, :] = fgw[1 - core].astype(F32).reshape(512, 128)
    store_other = fetch(gw_ref.at[other], gw_hbm.at[other], 14)

    for copy in (store_rows, store_cols, store_pair, store_b, store_wl, store_wr, store_mine, store_other):
        copy.wait()
    sent(rbuf.at[pl.ds(0, NQ - 1)], 0)
    sent(lbuf.at[pl.ds(0, NK - 1)], 1)
    sent(bsend, 2)
    sent(rdl.at[pl.ds(0, NK - 1)], 3)
    sent(bxy.at[pl.ds(0, NXY - 1)], 4)
    sent(rdr.at[pl.ds(0, NQ - 1)], 5)
    sent(rgc, 6)
    sent(rgx.at[pl.ds(0, NXY - 1)], 7)
    sent(bz.at[pl.ds(0, NZ - 1)], 8)
    sent(ssm, 9)
    sent(rsx.at[pl.ds(0, NXY - 1)], 10)
    sent(rgz.at[pl.ds(0, NZ - 1)], 11)
    sent(rsz.at[pl.ds(0, NZ - 1)], 12)
    sent(fgw.at[0, pl.ds(0, NXY - 1)], 13)
    sent(fsm.at[0], 14)
    sent(fgw.at[0], 15)


SCRATCH = (
    ((3, 16, 256), BF16),
    ((2, 64, 256), BF16),
    ((32, 256), BF16),
    ((32, 256), BF16),
    ((1024, 128), BF16),
    ((1, 128), F32),
    ((3, 16, 256), BF16),
    ((2, 64, 256), BF16),
    ((1024, 128), F32),
    ((1, 128), F32),
    ((96, 64, 128), BF16),
    ((96, 8192), BF16),
    ((6144, 128), F32),
    ((96, 64, 128), BF16),
    ((128, 4096), BF16),
    ((128, 256), BF16),
    ((48, 256), F32),
    ((128, 256), F32),
    ((48, 128), F32),
    ((128, 128), F32),
    ((256, 128), F32),
    ((1024, 128), BF16),
    ((32, 1024), BF16),
    ((512, 8192), BF16),
    ((4, 256, 4096), BF16),
    ((512, 128), F32),
    ((4, 96, 128), F32),
    ((96, 512), BF16),
    ((512, 96), BF16),
    ((4, 96, 128), F32),
    ((512, 128), F32),
    ((256, 128), F32),
    ((32, 4096), F32),
    ((NQ, 32, 128), BF16),
    ((NK, 16, 128), BF16),
    ((NK, 16, 128), BF16),
    ((NK, 16, 128), BF16),
    ((NQ, 32, 128), BF16),
    ((NQ, 32, 128), BF16),
    ((8, 128), F32),
    ((8, 128), F32),
    ((NXY, 8, 128), F32),
    ((NZ, 8, 128), F32),
    ((32, 2048), BF16),
    ((32, 2048), BF16),
    ((NXY, 32, 128), BF16),
    ((NXY, 32, 128), BF16),
    ((NZ, 32, 128), BF16),
    ((2, NXY, 32, 128), BF16),
    ((2, 32, 256), F32),
    ((32, 256), BF16),
    ((32, 256), BF16),
    ((NXY, 32, 256), BF16),
    ((NZ, 32, 256), BF16),
    ((2, 32, 256), F32),
)
SENDS = 16


OUTS = (
    ((96, 64, 128), BF16),
    ((3, 16, 256), BF16),
    ((2, 64, 256), BF16),
    ((1024, 128), F32),
    ((1, 128), F32),
    ((32, 256), F32),
    ((32, 256), F32),
)


def hand_over(*refs):
    n = len(OUTS)
    given, taken, held, insem, outsem = refs[:n], refs[n : 2 * n], refs[2 * n : 3 * n], refs[-2], refs[-1]
    pieces = [(0, pl.ds(k * 24, 24)) for k in range(4)] + [(k, None) for k in range(1, n)]
    loads, stores = [], []
    for m, (k, part) in enumerate(pieces):
        source, slot, target = (r[k] if part is None else r[k].at[part] for r in (given, held, taken))
        loads.append(pltpu.make_async_copy(source, slot, insem.at[m]))
        stores.append(pltpu.make_async_copy(slot, target, outsem.at[m]))
    for load in loads:
        load.start()
    for load, store in zip(loads, stores):
        load.wait()
        store.start()
    for store in stores:
        store.wait()


def local(xs, xc, w1, w2, w, b, g):
    hbm = pl.BlockSpec(memory_space=pl.ANY)
    outs = tuple(jax.ShapeDtypeStruct(shape, dtype) for shape, dtype in OUTS)
    found = pl.pallas_call(
        kernel,
        out_shape=outs,
        in_specs=[hbm] * 7,
        out_specs=(hbm,) * 7,
        scratch_shapes=[pltpu.VMEM(shape, dtype) for shape, dtype in SCRATCH]
        + [pltpu.SemaphoreType.DMA((15,))]
        + [pltpu.SemaphoreType.DMA((SENDS,))] * 2,
        compiler_params=pltpu.CompilerParams(
            collective_id=0, has_side_effects=True, vmem_limit_bytes=56 << 20
        ),
        cost_estimate=pl.CostEstimate(flops=3_300_000_000, bytes_accessed=5_000_000, transcendentals=0),
    )(jnp.transpose(xs, (1, 0, 2)), xc, w1.T, w2.T, w, b.reshape(1, 128), g)
    pair, grows, gcols, gw, gb, gwl, gwr = pl.pallas_call(
        hand_over,
        out_shape=outs,
        in_specs=[hbm] * 7,
        out_specs=(hbm,) * 7,
        scratch_shapes=[pltpu.VMEM(shape, dtype) for shape, dtype in OUTS]
        + [pltpu.SemaphoreType.DMA((len(OUTS) + 3,))] * 2,
    )(*found)
    return pair, jnp.transpose(grows, (1, 0, 2)), gcols, gw, gb.reshape(128), gwl.T, gwr.T


def solution(mesh):
    return jax.shard_map(
        local,
        mesh=mesh,
        in_specs=(
            P(None, ("qrow", "kcol"), None),
            P("qrow", "kcol", None),
            P(),
            P(),
            P(),
            P(),
            P("qrow", "kcol", None),
        ),
        out_specs=(
            P("qrow", "kcol", None),
            P(None, ("qrow", "kcol"), None),
            P("qrow", "kcol", None),
            P(),
            P(),
            P(),
            P(),
        ),
        check_vma=False,
    )
```

```python
import jax
import jax.numpy as jnp
from jax import lax
from jax.experimental import pallas as pl
from jax.experimental.pallas import tpu as pltpu
from jax.sharding import PartitionSpec as P

F32, BF16 = jnp.float32, jnp.bfloat16
MESH = pl.DeviceIdType.MESH
EPS = 1e-05

NQ, NZ, NC, NXY, NW = 8, 8, 4, 16, 16


def nn(a, b):
    return jnp.dot(a, b, preferred_element_type=F32)


def nt(a, b):
    return lax.dot_general(a, b, (((1,), (1,)), ((), ())), preferred_element_type=F32)


def mean_of(v):
    return jnp.mean(v, axis=-1, keepdims=True)


def normalize(v):
    center = v - mean_of(v)
    inv = lax.rsqrt(mean_of(center * center) + EPS)
    return center * inv, inv


def norm_back(g, hat, inv):
    return inv * (g - mean_of(g) - hat * mean_of(g * hat))


def iota(shape, dim):
    return lax.broadcasted_iota(jnp.int32, shape, dim)


def loop(lo, hi, body):
    def step(d, carry):
        body(d)
        return carry

    lax.fori_loop(lo, hi, step, 0)


def kernel(
    xs_hbm, xc_hbm, w1_hbm, w2_hbm, w_hbm, b_hbm, g_hbm,
    pair_hbm, grows_hbm, gcols_hbm, gw_hbm, gb_hbm, gwl_hbm, gwr_hbm,
    xs_ref, xc_ref, w1_ref, w2_ref, w_ref, b_ref, grows_ref, gcols_ref, gw_ref, gb_ref,
    g, gs, pf, po, w4, w2r, hat_r, hat_c, inv_r, inv_c,
    rf, rm, rl, ap, bp, lf, lmf, lm, lt, dlf, dsf, drf, gwp,
    rbuf, lbuf, sdl, rdl, szl, rzl, sdr, rdr,
    bsend, bcore, bxy, bz,
    sgc, rgc, sgx, rgx, rgz, fgw,
    ssm, rsx, rsz, fsm, gsm_ref,
    lsem, ssem, rsem,
):
    me_q, me_k = lax.axis_index("qrow"), lax.axis_index("kcol")
    me_z = lax.div(me_k, 4)
    me_x = lax.rem(lax.div(me_k, 2), 2)
    core = lax.rem(me_k, 2)
    me_p = me_x * 8 + me_q
    me_c = me_x * 2 + core
    me_w = me_z * 2 + core

    def at_c(d):
        c = lax.rem(me_c + d, NC)
        return c, (me_q, me_z * 4 + c)

    def at_q(d):
        q = lax.rem(me_q + d, NQ)
        return q, (q, me_k)

    def at_p(d):
        p = lax.rem(me_p + d, NXY)
        return p, (lax.rem(p, 8), me_z * 4 + lax.div(p, 8) * 2 + core)

    def at_z(d):
        z = lax.rem(me_z + d, NZ)
        return z, (me_q, z * 4 + me_x * 2 + core)

    def at_zc(d):
        w = lax.rem(me_w + d, NW)
        return w, (me_q, lax.div(w, 2) * 4 + me_x * 2 + lax.rem(w, 2))

    mate = (me_q, me_k + 1 - 2 * core)

    def send(src, dst, n, device):
        pltpu.make_async_remote_copy(
            src_ref=src, dst_ref=dst, send_sem=ssem.at[n], recv_sem=rsem.at[n],
            device_id=device, device_id_type=MESH,
        ).start()

    def arrived(ref, n):
        pltpu.make_async_copy(ref, ref, rsem.at[n]).wait()

    def sent(ref, n):
        pltpu.make_async_copy(ref, ref, ssem.at[n]).wait()

    def fetch(src, dst, n):
        copy = pltpu.make_async_copy(src, dst, lsem.at[n])
        copy.start()
        return copy

    load_xc = fetch(xc_hbm, xc_ref, 0)
    load_w2 = fetch(w2_hbm, w2_ref, 1)
    load_xs = fetch(xs_hbm, xs_ref, 2)
    load_w1 = fetch(w1_hbm, w1_ref, 3)
    load_g = fetch(g_hbm, g, 4)
    load_w = fetch(w_hbm, w_ref, 5)
    load_b = fetch(b_hbm, b_ref, 6)

    barrier = pltpu.get_barrier_semaphore()

    def greet(device):
        pl.semaphore_signal(barrier, inc=1, device_id=device, device_id_type=MESH)

    loop(1, NW, lambda d: greet(at_zc(d)[1]))
    loop(1, NXY, lambda d: greet(at_p(d)[1]))
    greet((me_q, me_z * 4 + 3 - me_c))

    lane_group = lax.shift_right_logical(iota((16, 128), 1), 5)
    lane_s = jnp.bitwise_and(iota((16, 512), 1), 15) == iota((16, 512), 0)
    fold = (lax.shift_right_logical(iota((128, 512), 1), 4) == iota((128, 512), 0)).astype(BF16)

    load_xc.wait()
    load_w2.wait()
    for jg in range(4):
        w2r[jg * 32 : (jg + 1) * 32, :] = w2_ref[...]
    hat, inv = normalize(xc_ref[...].astype(F32).reshape(128, 256))
    hat_c[...] = hat
    inv_c[...] = jnp.broadcast_to(inv, (128, 128))
    right = nt(hat.astype(BF16), w2r[...]).astype(BF16).astype(F32)
    tiles = []
    for t in range(2):
        tile = right[t * 64 : t * 64 + 16, :]
        for jg in range(1, 4):
            tile = jnp.where(lane_group == jg, right[t * 64 + jg * 16 : t * 64 + jg * 16 + 16, :], tile)
        tiles.append(tile)
    rbuf[me_q] = jnp.concatenate(tiles, axis=0).astype(BF16)

    pl.semaphore_wait(barrier, NW + NXY - 1)
    loop(1, NQ, lambda d: send(rbuf.at[me_q], rbuf.at[me_q], 0, at_q(d)[1]))

    load_xs.wait()
    load_w1.wait()
    hat, inv = normalize(xs_ref[...].astype(F32).reshape(48, 256))
    hat_r[...] = hat
    inv_r[...] = jnp.broadcast_to(inv, (48, 128))
    left = nt(hat.astype(BF16), w1_ref[...]).astype(BF16)
    tile = jnp.zeros((16, 128), F32)
    for i3 in range(3):
        wide = nn(left[i3 * 16 : i3 * 16 + 16, :], fold[0:32, :])
        row = jnp.sum(jnp.where(lane_s, wide, 0.0), axis=0, keepdims=True)
        for cq in range(4):
            piece = jnp.broadcast_to(row[:, cq * 128 : (cq + 1) * 128], (16, 128))
            tile = jnp.where(iota((16, 128), 0) == i3 * 4 + cq, piece, tile)
    lbuf[me_c, me_z] = tile.astype(BF16)

    loop(1, NZ, lambda d: send(lbuf.at[me_c, me_z], lbuf.at[me_c, me_z], 1, at_z(d)[1]))

    load_w.wait()
    for c in range(32):
        block = w_ref[c * 32 : (c + 1) * 32, :]
        for jg in range(4):
            w4[jg * 32 : (jg + 1) * 32, c * 128 : (c + 1) * 128] = block

    load_g.wait()

    def widen(n, total):
        for u in range(4):
            v = g[4 * n + u].astype(F32)
            pf[pl.ds(pl.multiple_of((4 * n + u) * 64, 64), 64), :] = v
            total = total + v
        return total

    total = lax.fori_loop(0, 24, widen, jnp.zeros((64, 128), F32))
    bsend[...] = jnp.broadcast_to(jnp.sum(total, axis=0, keepdims=True), (8, 128))

    def turn(n):
        for u in range(4):
            lanes = pl.ds(pl.multiple_of((4 * n + u) * 128, 128), 128)
            gs[:, lanes] = pf[pl.ds(4 * n + u, 96, stride=64), :].astype(BF16)

    loop(0, 16, turn)
    send(bsend, bcore, 2, mate)

    arrived(rbuf.at[pl.ds(0, NQ - 1)], 0)
    for s in range(16):
        part = rbuf[s // 2, (s % 2) * 16 : (s % 2) * 16 + 16, :].astype(F32)
        rf[pl.ds(s, 16, stride=16), :] = part * (1.0 / 16.0)
    rx = rf[...]
    group = lax.shift_right_logical(iota((256, 128), 1), 5)
    for jg in range(4):
        rm[jg * 256 : (jg + 1) * 256, :] = jnp.where(group == jg, rx, 0.0).astype(BF16)
    rxt = rx.T
    for jg in range(4):
        rl[:, jg * 256 : (jg + 1) * 256] = rxt[jg * 32 : (jg + 1) * 32, :].astype(BF16)

    def make_a(jg):
        for cc in range(16):
            r = nn(
                rm[pl.ds(pl.multiple_of(jg * 256, 256), 256), :],
                w4[:, cc * 256 : (cc + 1) * 256],
            ).astype(BF16)
            for j in range(16):
                lanes = pl.ds(pl.multiple_of((jg * 16 + j) * 128, 128), 128)
                for h in range(2):
                    to = cc * 32 + h * 16
                    ap[to : to + 16, lanes] = r[j * 16 : (j + 1) * 16, h * 128 : (h + 1) * 128]

    loop(0, 4, make_a)

    arrived(lbuf.at[0, pl.ds(0, NZ - 1)], 1)
    loop(1, NC, lambda d: send(lbuf.at[me_c], lbuf.at[me_c], 16, at_c(d)[1]))

    dl = nt(ap[...], gs[...])
    for cq in range(4):
        dlf[cq] = dl[cq * 128 : (cq + 1) * 128, :].T
    dsf[...] = jnp.zeros((512, 128), F32)
    for c in range(4):
        for i3 in range(3):
            for cq in range(4):
                part = dlf[cq, pl.ds(c * 3 + i3, 8, stride=12), :]
                dsf[pl.ds(c * 128 + i3 * 4 + cq, 8, stride=16), :] = part
    sdl[...] = dsf[...].astype(BF16).reshape(4, 8, 16, 128)
    rdl[me_c] = sdl[me_c]

    def send_dl(d):
        c, device = at_c(d)
        send(sdl.at[c], rdl.at[me_c], 3, device)

    loop(1, NC, send_dl)

    arrived(lbuf.at[pl.ds(0, NC - 1)], 16)
    lf[...] = lbuf[...].astype(F32).reshape(512, 128)
    for c in range(4):
        for i3 in range(3):
            for cq in range(4):
                part = lf[pl.ds(c * 128 + i3 * 4 + cq, 8, stride=16), :]
                lmf[cq, pl.ds(c * 3 + i3, 8, stride=12), :] = part
    for cq in range(4):
        lm[:, cq * 128 : (cq + 1) * 128] = lmf[cq].astype(BF16)
        lt[cq * 128 : (cq + 1) * 128, :] = lmf[cq].T.astype(BF16)

    arrived(bcore, 2)
    bxy[me_p] = bsend[...] + bcore[...]
    loop(1, NXY, lambda d: send(bxy.at[me_p], bxy.at[me_p], 4, at_p(d)[1]))

    def make_b(jg):
        for p in range(8):
            lanes = pl.ds(pl.multiple_of(jg * 2048 + p * 256, 256), 256)
            r = nn(lt[...], gs[:, lanes]).astype(BF16)
            for c in range(32):
                for h in range(2):
                    to = (p * 2 + h) * 16
                    bp[jg, to : to + 16, c * 128 : (c + 1) * 128] = r[c * 16 : (c + 1) * 16, h * 128 : (h + 1) * 128]

    loop(0, 4, make_b)

    arrived(rdl.at[pl.ds(0, NC - 1)], 3)
    total = rdl[0].astype(F32)
    for c in range(1, NC):
        total = total + rdl[c].astype(F32)
    szl[...] = total.astype(BF16)
    rzl[me_z] = szl[me_z]

    def send_zl(d):
        z, device = at_z(d)
        send(szl.at[z], rzl.at[me_z], 17, device)

    loop(1, NZ, send_zl)

    dr = jnp.zeros((256, 128), F32)
    for jg in range(4):
        dr = dr + jnp.where(group == jg, nt(bp[jg], w4[...]), 0.0)
    drf[...] = dr * (1.0 / 16.0)
    for s in range(16):
        sdr[s // 2, (s % 2) * 16 : (s % 2) * 16 + 16, :] = drf[pl.ds(s, 16, stride=16), :].astype(BF16)
    rdr[me_q] = sdr[me_q]

    def send_dr(d):
        q, device = at_q(d)
        send(sdr.at[q], rdr.at[me_q], 5, device)

    loop(1, NQ, send_dr)

    def make_gw(n):
        lanes = pl.ds(pl.multiple_of(lax.rem(n + 2 - 2 * core, 4) * 1024, 1024), 1024)
        gwp[:, lanes] = nn(rl[...], bp[:, :, lanes].reshape(1024, 1024))

        @pl.when(n == 1)
        def _():
            sgc[...] = gwp[:, pl.ds(pl.multiple_of((1 - core) * 2048, 2048), 2048)].astype(BF16)
            send(sgc, rgc, 6, mate)

    loop(0, 4, make_gw)

    arrived(rgc, 6)
    for p in range(16):
        lanes = pl.ds(pl.multiple_of(core * 2048 + p * 128, 128), 128)
        half = gwp[:, lanes] + rgc[:, p * 128 : (p + 1) * 128].astype(F32)
        sgx[p] = half.astype(BF16)
    rgx[me_p] = sgx[me_p]

    def send_gx(d):
        p, device = at_p(d)
        send(sgx.at[p], rgx.at[me_p], 7, device)

    loop(1, NXY, send_gx)

    def tiled(v, first):
        for n in range(8):
            ssm[first + n] = v[n // 2 * 8 : n // 2 * 8 + 8, n % 2 * 128 : n % 2 * 128 + 128]

    arrived(rzl.at[pl.ds(0, NZ - 1)], 17)
    dsum = rzl[0].astype(F32)
    for z in range(1, NZ):
        dsum = dsum + rzl[z].astype(F32)
    dsum = dsum.astype(BF16).astype(F32)
    parts = []
    for i3 in range(3):
        row = jnp.concatenate([dsum[i3 * 4 + cq : i3 * 4 + cq + 1, :] for cq in range(4)], axis=1)
        parts.append(jnp.where(lane_s, jnp.broadcast_to(row, (16, 512)), 0.0))
    dleft = nt(jnp.concatenate(parts, axis=0).astype(BF16), fold)
    hat = hat_r[...]
    tiled(nn(dleft.T[0:32, :].astype(BF16), hat.astype(BF16)), 0)
    back = nn(dleft[:, 0:32].astype(BF16), w1_ref[...])
    out = norm_back(back, hat, inv_r[:, 0:1])
    grows_ref[...] = out.reshape(3, 16, 256).astype(BF16)
    store_rows = fetch(grows_ref, grows_hbm, 7)

    arrived(bxy.at[pl.ds(0, NXY - 1)], 4)
    total = bxy[0]
    for p in range(1, NXY):
        total = total + bxy[p]
    bz[me_z] = total
    loop(1, NZ, lambda d: send(bz.at[me_z], bz.at[me_z], 8, at_z(d)[1]))

    arrived(rdr.at[pl.ds(0, NQ - 1)], 5)
    dsum = rdr[0].astype(F32)
    for q in range(1, NQ):
        dsum = dsum + rdr[q].astype(F32)
    dsum = dsum.astype(BF16).astype(F32)
    parts = []
    for t in range(2):
        for jg in range(4):
            parts.append(jnp.where(lane_group == jg, dsum[t * 16 : t * 16 + 16, :], 0.0))
    dright = jnp.concatenate(parts, axis=0)
    hat = hat_c[...]
    term = nn(dright.T.astype(BF16), hat.astype(BF16))
    term = term[0:32, :] + term[32:64, :] + term[64:96, :] + term[96:128, :]
    tiled(term, 8)
    rsx[me_p] = ssm[me_p]

    def send_small(d):
        p, device = at_p(d)
        send(ssm.at[p], rsx.at[me_p], 9, device)

    loop(1, NXY, send_small)
    back = nn(dright.astype(BF16), w2r[...])
    out = norm_back(back, hat, inv_c[:, 0:1])
    gcols_ref[...] = out.reshape(2, 64, 256).astype(BF16)
    store_cols = fetch(gcols_ref, gcols_hbm, 8)

    def make_p(jg):
        for p in range(8):
            lanes = pl.ds(pl.multiple_of(jg * 2048 + p * 256, 256), 256)
            r = nn(lm[...], ap[:, lanes])
            for h in range(2):
                pf[pl.ds(jg * 16 + 2 * p + h, 96, stride=64), :] = r[:, h * 128 : (h + 1) * 128]

    loop(0, 4, make_p)

    load_b.wait()
    bias = b_ref[...]

    def finish(n):
        for u in range(4):
            rows = pf[pl.ds(pl.multiple_of((4 * n + u) * 64, 64), 64), :]
            po[4 * n + u] = (rows + bias).astype(BF16)

    loop(0, 24, finish)
    store_pair = fetch(po, pair_hbm, 9)

    arrived(rgx.at[pl.ds(0, NXY - 1)], 7)
    total = rgx[0].astype(F32)
    for p in range(1, NXY):
        total = total + rgx[p].astype(F32)
    rgz[me_z] = total.astype(BF16)
    loop(1, NZ, lambda d: send(rgz.at[me_z], rgz.at[me_z], 11, at_z(d)[1]))

    arrived(rsx.at[pl.ds(0, NXY - 1)], 9)
    total = rsx[0]
    for p in range(1, NXY):
        total = total + rsx[p]
    rsz[me_w] = total
    loop(1, NW, lambda d: send(rsz.at[me_w], rsz.at[me_w], 10, at_zc(d)[1]))

    arrived(rgz.at[pl.ds(0, NZ - 1)], 11)
    total = rgz[0].astype(F32)
    for z in range(1, NZ):
        total = total + rgz[z].astype(F32)
    fgw[core, me_p] = total.astype(BF16)
    loop(1, NXY, lambda d: send(fgw.at[core, me_p], fgw.at[core, me_p], 13, at_p(d)[1]))

    arrived(rsz.at[pl.ds(0, NW - 1)], 10)
    total = rsz[0]
    for w in range(1, NW):
        total = total + rsz[w]
    fsm[me_p] = total
    loop(1, NXY, lambda d: send(fsm.at[me_p], fsm.at[me_p], 14, at_p(d)[1]))

    arrived(bz.at[pl.ds(0, NZ - 1)], 8)
    total = bz[0]
    for z in range(1, NZ):
        total = total + bz[z]
    gb_ref[...] = total[0:1, :]
    store_b = fetch(gb_ref, gb_hbm, 10)

    arrived(fgw.at[0, pl.ds(0, NXY - 1)], 13)
    send(fgw.at[core], fgw.at[core], 15, mate)
    mine = pl.ds(pl.multiple_of(core * 512, 512), 512)
    gw_ref[mine, :] = fgw[core].astype(F32).reshape(512, 128)
    store_mine = fetch(gw_ref.at[mine], gw_hbm.at[mine], 15)
    arrived(fsm.at[pl.ds(0, NXY - 1)], 14)
    for n in range(16):
        gsm_ref[n // 8, n % 8 // 2 * 8 : n % 8 // 2 * 8 + 8, n % 2 * 128 : n % 2 * 128 + 128] = fsm[n]
    store_wl = fetch(gsm_ref.at[0], gwl_hbm, 11)
    store_wr = fetch(gsm_ref.at[1], gwr_hbm, 12)
    arrived(fgw.at[0], 15)
    other = pl.ds(pl.multiple_of((1 - core) * 512, 512), 512)
    gw_ref[other, :] = fgw[1 - core].astype(F32).reshape(512, 128)
    store_other = fetch(gw_ref.at[other], gw_hbm.at[other], 16)

    for copy in (store_rows, store_cols, store_pair, store_b, store_mine, store_other, store_wl, store_wr):
        copy.wait()
    sent(rbuf.at[pl.ds(0, NQ - 1)], 0)
    sent(lbuf.at[0, pl.ds(0, NZ - 1)], 1)
    sent(bsend, 2)
    sent(rdl.at[pl.ds(0, NC - 1)], 3)
    sent(bxy.at[pl.ds(0, NXY - 1)], 4)
    sent(rdr.at[pl.ds(0, NQ - 1)], 5)
    sent(rgc, 6)
    sent(rgx.at[pl.ds(0, NXY - 1)], 7)
    sent(bz.at[pl.ds(0, NZ - 1)], 8)
    sent(rsx.at[pl.ds(0, NXY - 1)], 9)
    sent(rsz.at[pl.ds(0, NW - 1)], 10)
    sent(rgz.at[pl.ds(0, NZ - 1)], 11)
    sent(fgw.at[0, pl.ds(0, NXY - 1)], 13)
    sent(fsm.at[pl.ds(0, NXY - 1)], 14)
    sent(fgw.at[0], 15)
    sent(lbuf.at[pl.ds(0, NC - 1)], 16)
    sent(rzl.at[pl.ds(0, NZ - 1)], 17)


SCRATCH = (
    ((3, 16, 256), BF16),
    ((2, 64, 256), BF16),
    ((32, 256), BF16),
    ((32, 256), BF16),
    ((1024, 128), BF16),
    ((1, 128), F32),
    ((3, 16, 256), BF16),
    ((2, 64, 256), BF16),
    ((1024, 128), F32),
    ((1, 128), F32),
    ((96, 64, 128), BF16),
    ((96, 8192), BF16),
    ((6144, 128), F32),
    ((96, 64, 128), BF16),
    ((128, 4096), BF16),
    ((128, 256), BF16),
    ((48, 256), F32),
    ((128, 256), F32),
    ((48, 128), F32),
    ((128, 128), F32),
    ((256, 128), F32),
    ((1024, 128), BF16),
    ((32, 1024), BF16),
    ((512, 8192), BF16),
    ((4, 256, 4096), BF16),
    ((512, 128), F32),
    ((4, 96, 128), F32),
    ((96, 512), BF16),
    ((512, 96), BF16),
    ((4, 96, 128), F32),
    ((512, 128), F32),
    ((256, 128), F32),
    ((32, 4096), F32),
    ((NQ, 32, 128), BF16),
    ((NC, NZ, 16, 128), BF16),
    ((NC, NZ, 16, 128), BF16),
    ((NC, NZ, 16, 128), BF16),
    ((NZ, 16, 128), BF16),
    ((NZ, 16, 128), BF16),
    ((NQ, 32, 128), BF16),
    ((NQ, 32, 128), BF16),
    ((8, 128), F32),
    ((8, 128), F32),
    ((NXY, 8, 128), F32),
    ((NZ, 8, 128), F32),
    ((32, 2048), BF16),
    ((32, 2048), BF16),
    ((NXY, 32, 128), BF16),
    ((NXY, 32, 128), BF16),
    ((NZ, 32, 128), BF16),
    ((2, NXY, 32, 128), BF16),
    ((NXY, 8, 128), F32),
    ((NXY, 8, 128), F32),
    ((NW, 8, 128), F32),
    ((NXY, 8, 128), F32),
    ((2, 32, 256), F32),
)
SENDS = 18


OUTS = (
    ((96, 64, 128), BF16),
    ((3, 16, 256), BF16),
    ((2, 64, 256), BF16),
    ((1024, 128), F32),
    ((1, 128), F32),
    ((32, 256), F32),
    ((32, 256), F32),
)


def hand_over(*refs):
    n = len(OUTS)
    given, taken, held, insem, outsem = refs[:n], refs[n : 2 * n], refs[2 * n : 3 * n], refs[-2], refs[-1]
    pieces = [(0, pl.ds(k * 24, 24)) for k in range(4)] + [(k, None) for k in range(1, n)]
    loads, stores = [], []
    for m, (k, part) in enumerate(pieces):
        source, slot, target = (r[k] if part is None else r[k].at[part] for r in (given, held, taken))
        loads.append(pltpu.make_async_copy(source, slot, insem.at[m]))
        stores.append(pltpu.make_async_copy(slot, target, outsem.at[m]))
    for load in loads:
        load.start()
    for load, store in zip(loads, stores):
        load.wait()
        store.start()
    for store in stores:
        store.wait()


def local(xs, xc, w1, w2, w, b, g):
    hbm = pl.BlockSpec(memory_space=pl.ANY)
    outs = tuple(jax.ShapeDtypeStruct(shape, dtype) for shape, dtype in OUTS)
    found = pl.pallas_call(
        kernel,
        out_shape=outs,
        in_specs=[hbm] * 7,
        out_specs=(hbm,) * 7,
        scratch_shapes=[pltpu.VMEM(shape, dtype) for shape, dtype in SCRATCH]
        + [pltpu.SemaphoreType.DMA((17,))]
        + [pltpu.SemaphoreType.DMA((SENDS,))] * 2,
        compiler_params=pltpu.CompilerParams(
            collective_id=0, has_side_effects=True, vmem_limit_bytes=56 << 20
        ),
        cost_estimate=pl.CostEstimate(flops=3_300_000_000, bytes_accessed=5_000_000, transcendentals=0),
    )(jnp.transpose(xs, (1, 0, 2)), xc, w1.T, w2.T, w, b.reshape(1, 128), g)
    pair, grows, gcols, gw, gb, gwl, gwr = pl.pallas_call(
        hand_over,
        out_shape=outs,
        in_specs=[hbm] * 7,
        out_specs=(hbm,) * 7,
        scratch_shapes=[pltpu.VMEM(shape, dtype) for shape, dtype in OUTS]
        + [pltpu.SemaphoreType.DMA((len(OUTS) + 3,))] * 2,
    )(*found)
    return pair, jnp.transpose(grows, (1, 0, 2)), gcols, gw, gb.reshape(128), gwl.T, gwr.T


def solution(mesh):
    return jax.shard_map(
        local,
        mesh=mesh,
        in_specs=(
            P(None, ("qrow", "kcol"), None),
            P("qrow", "kcol", None),
            P(),
            P(),
            P(),
            P(),
            P("qrow", "kcol", None),
        ),
        out_specs=(
            P("qrow", "kcol", None),
            P(None, ("qrow", "kcol"), None),
            P("qrow", "kcol", None),
            P(),
            P(),
            P(),
            P(),
        ),
        check_vma=False,
    )
```

```python
import jax
import jax.numpy as jnp
from jax import lax
from jax.experimental import pallas as pl
from jax.experimental.pallas import tpu as pltpu
from jax.sharding import PartitionSpec as P

F32, BF16 = jnp.float32, jnp.bfloat16
MESH = pl.DeviceIdType.MESH
EPS = 1e-05

NQ, NZ, NC, NXY, NW = 8, 8, 4, 16, 16


def nn(a, b):
    return jnp.dot(a, b, preferred_element_type=F32)


def nt(a, b):
    return lax.dot_general(a, b, (((1,), (1,)), ((), ())), preferred_element_type=F32)


def mean_of(v):
    return jnp.mean(v, axis=-1, keepdims=True)


def normalize(v):
    center = v - mean_of(v)
    inv = lax.rsqrt(mean_of(center * center) + EPS)
    return center * inv, inv


def norm_back(g, hat, inv):
    return inv * (g - mean_of(g) - hat * mean_of(g * hat))


def iota(shape, dim):
    return lax.broadcasted_iota(jnp.int32, shape, dim)


def loop(lo, hi, body):
    def step(d, carry):
        body(d)
        return carry

    lax.fori_loop(lo, hi, step, 0)


def kernel(
    xs_hbm, xc_hbm, w1_hbm, w2_hbm, w_hbm, b_hbm, g_hbm,
    pair_hbm, grows_hbm, gcols_hbm, gw_hbm, gb_hbm, gwl_hbm, gwr_hbm,
    xs_ref, xc_ref, w1_ref, w2_ref, w_ref, b_ref, grows_ref, gcols_ref, gw_ref, gb_ref,
    g, gs, pf, po, w4, w2r, hat_r, hat_c, inv_r, inv_c,
    rf, rm, rl, ap, bp, lf, lmf, lm, lt, dlf, dsf, drf, gwp,
    rbuf, lbuf, sdl, rdl, szl, rzl, sdr, rdr,
    bsend, bcore, bxy, bz,
    sgc, rgc, sgx, rgx, rgz, fgw,
    ssm, rsx, rsz, fsm, gsm_ref,
    lsem, ssem, rsem,
):
    me_q, me_k = lax.axis_index("qrow"), lax.axis_index("kcol")
    me_z = lax.div(me_k, 4)
    me_x = lax.rem(lax.div(me_k, 2), 2)
    core = lax.rem(me_k, 2)
    me_p = me_x * 8 + me_q
    me_c = me_x * 2 + core
    me_w = me_z * 2 + core

    def at_c(d):
        c = lax.rem(me_c + d, NC)
        return c, (me_q, me_z * 4 + c)

    def at_q(d):
        q = lax.rem(me_q + d, NQ)
        return q, (q, me_k)

    def at_p(d):
        p = lax.rem(me_p + d, NXY)
        return p, (lax.rem(p, 8), me_z * 4 + lax.div(p, 8) * 2 + core)

    def at_z(d):
        z = lax.rem(me_z + d, NZ)
        return z, (me_q, z * 4 + me_x * 2 + core)

    def at_zc(d):
        w = lax.rem(me_w + d, NW)
        return w, (me_q, lax.div(w, 2) * 4 + me_x * 2 + lax.rem(w, 2))

    mate = (me_q, me_k + 1 - 2 * core)

    def send(src, dst, n, device):
        pltpu.make_async_remote_copy(
            src_ref=src, dst_ref=dst, send_sem=ssem.at[n], recv_sem=rsem.at[n],
            device_id=device, device_id_type=MESH,
        ).start()

    def arrived(ref, n):
        pltpu.make_async_copy(ref, ref, rsem.at[n]).wait()

    def sent(ref, n):
        pltpu.make_async_copy(ref, ref, ssem.at[n]).wait()

    def fetch(src, dst, n):
        copy = pltpu.make_async_copy(src, dst, lsem.at[n])
        copy.start()
        return copy

    load_xc = fetch(xc_hbm, xc_ref, 0)
    load_w2 = fetch(w2_hbm, w2_ref, 1)
    load_xs = fetch(xs_hbm, xs_ref, 2)
    load_w1 = fetch(w1_hbm, w1_ref, 3)
    load_g = fetch(g_hbm, g, 4)
    load_w = fetch(w_hbm, w_ref, 5)
    load_b = fetch(b_hbm, b_ref, 6)

    barrier = pltpu.get_barrier_semaphore()

    def greet(device):
        pl.semaphore_signal(barrier, inc=1, device_id=device, device_id_type=MESH)

    loop(1, NW, lambda d: greet(at_zc(d)[1]))
    loop(1, NXY, lambda d: greet(at_p(d)[1]))
    greet((me_q, me_z * 4 + 3 - me_c))

    lane_group = lax.shift_right_logical(iota((16, 128), 1), 5)
    lane_s = jnp.bitwise_and(iota((16, 512), 1), 15) == iota((16, 512), 0)
    fold = (lax.shift_right_logical(iota((128, 512), 1), 4) == iota((128, 512), 0)).astype(BF16)

    load_xc.wait()
    load_w2.wait()
    for jg in range(4):
        w2r[jg * 32 : (jg + 1) * 32, :] = w2_ref[...]
    hat, inv = normalize(xc_ref[...].astype(F32).reshape(128, 256))
    hat_c[...] = hat
    inv_c[...] = jnp.broadcast_to(inv, (128, 128))
    right = nt(hat.astype(BF16), w2r[...]).astype(BF16).astype(F32)
    tiles = []
    for t in range(2):
        tile = right[t * 64 : t * 64 + 16, :]
        for jg in range(1, 4):
            tile = jnp.where(lane_group == jg, right[t * 64 + jg * 16 : t * 64 + jg * 16 + 16, :], tile)
        tiles.append(tile)
    rbuf[me_q] = jnp.concatenate(tiles, axis=0).astype(BF16)

    pl.semaphore_wait(barrier, NW + NXY - 1)
    loop(1, NQ, lambda d: send(rbuf.at[me_q], rbuf.at[me_q], 0, at_q(d)[1]))

    load_xs.wait()
    load_w1.wait()
    hat, inv = normalize(xs_ref[...].astype(F32).reshape(48, 256))
    hat_r[...] = hat
    inv_r[...] = jnp.broadcast_to(inv, (48, 128))
    left = nt(hat.astype(BF16), w1_ref[...]).astype(BF16)
    tile = jnp.zeros((16, 128), F32)
    for i3 in range(3):
        wide = nn(left[i3 * 16 : i3 * 16 + 16, :], fold[0:32, :])
        row = jnp.sum(jnp.where(lane_s, wide, 0.0), axis=0, keepdims=True)
        for cq in range(4):
            piece = jnp.broadcast_to(row[:, cq * 128 : (cq + 1) * 128], (16, 128))
            tile = jnp.where(iota((16, 128), 0) == i3 * 4 + cq, piece, tile)
    lbuf[me_c, me_z] = tile.astype(BF16)

    loop(1, NZ, lambda d: send(lbuf.at[me_c, me_z], lbuf.at[me_c, me_z], 1, at_z(d)[1]))

    load_w.wait()
    for c in range(32):
        block = w_ref[c * 32 : (c + 1) * 32, :]
        for jg in range(4):
            w4[jg * 32 : (jg + 1) * 32, c * 128 : (c + 1) * 128] = block

    load_g.wait()

    def widen(n, total):
        for u in range(4):
            v = g[4 * n + u].astype(F32)
            pf[pl.ds(pl.multiple_of((4 * n + u) * 64, 64), 64), :] = v
            total = total + v
        return total

    total = lax.fori_loop(0, 24, widen, jnp.zeros((64, 128), F32))
    bsend[...] = jnp.broadcast_to(jnp.sum(total, axis=0, keepdims=True), (8, 128))

    def turn(n):
        for u in range(4):
            lanes = pl.ds(pl.multiple_of((4 * n + u) * 128, 128), 128)
            gs[:, lanes] = pf[pl.ds(4 * n + u, 96, stride=64), :].astype(BF16)

    loop(0, 16, turn)
    send(bsend, bcore, 2, mate)

    arrived(rbuf.at[pl.ds(0, NQ - 1)], 0)
    for s in range(16):
        part = rbuf[s // 2, (s % 2) * 16 : (s % 2) * 16 + 16, :].astype(F32)
        rf[pl.ds(s, 16, stride=16), :] = part * (1.0 / 16.0)
    rx = rf[...]
    group = lax.shift_right_logical(iota((256, 128), 1), 5)
    for jg in range(4):
        rm[jg * 256 : (jg + 1) * 256, :] = jnp.where(group == jg, rx, 0.0).astype(BF16)
    rxt = rx.T
    for jg in range(4):
        rl[:, jg * 256 : (jg + 1) * 256] = rxt[jg * 32 : (jg + 1) * 32, :].astype(BF16)

    def make_a(n):
        for u in range(2):
            jg = 2 * n + u
            for cc in range(16):
                r = nn(
                    rm[pl.ds(pl.multiple_of(jg * 256, 256), 256), :],
                    w4[:, cc * 256 : (cc + 1) * 256],
                ).astype(BF16)
                for j in range(16):
                    lanes = pl.ds(pl.multiple_of((jg * 16 + j) * 128, 128), 128)
                    for h in range(2):
                        to = cc * 32 + h * 16
                        ap[to : to + 16, lanes] = r[j * 16 : (j + 1) * 16, h * 128 : (h + 1) * 128]

    loop(0, 2, make_a)

    arrived(lbuf.at[0, pl.ds(0, NZ - 1)], 1)
    loop(1, NC, lambda d: send(lbuf.at[me_c], lbuf.at[me_c], 16, at_c(d)[1]))

    dl = nt(ap[...], gs[...])
    for cq in range(4):
        dlf[cq] = dl[cq * 128 : (cq + 1) * 128, :].T
    dsf[...] = jnp.zeros((512, 128), F32)
    for c in range(4):
        for i3 in range(3):
            for cq in range(4):
                part = dlf[cq, pl.ds(c * 3 + i3, 8, stride=12), :]
                dsf[pl.ds(c * 128 + i3 * 4 + cq, 8, stride=16), :] = part
    sdl[...] = dsf[...].astype(BF16).reshape(4, 8, 16, 128)
    rdl[me_c] = sdl[me_c]

    def send_dl(d):
        c, device = at_c(d)
        send(sdl.at[c], rdl.at[me_c], 3, device)

    loop(1, NC, send_dl)

    arrived(lbuf.at[pl.ds(0, NC - 1)], 16)
    lf[...] = lbuf[...].astype(F32).reshape(512, 128)
    for c in range(4):
        for i3 in range(3):
            for cq in range(4):
                part = lf[pl.ds(c * 128 + i3 * 4 + cq, 8, stride=16), :]
                lmf[cq, pl.ds(c * 3 + i3, 8, stride=12), :] = part
    for cq in range(4):
        lm[:, cq * 128 : (cq + 1) * 128] = lmf[cq].astype(BF16)
        lt[cq * 128 : (cq + 1) * 128, :] = lmf[cq].T.astype(BF16)

    arrived(bcore, 2)
    bxy[me_p] = bsend[...] + bcore[...]
    loop(1, NXY, lambda d: send(bxy.at[me_p], bxy.at[me_p], 4, at_p(d)[1]))

    def make_b(n):
        for u in range(2):
            jg = 2 * n + u
            for p in range(8):
                lanes = pl.ds(pl.multiple_of(jg * 2048 + p * 256, 256), 256)
                r = nn(lt[...], gs[:, lanes]).astype(BF16)
                for c in range(32):
                    for h in range(2):
                        to = (p * 2 + h) * 16
                        bp[jg, to : to + 16, c * 128 : (c + 1) * 128] = r[c * 16 : (c + 1) * 16, h * 128 : (h + 1) * 128]

    loop(0, 2, make_b)

    arrived(rdl.at[pl.ds(0, NC - 1)], 3)
    total = rdl[0].astype(F32)
    for c in range(1, NC):
        total = total + rdl[c].astype(F32)
    szl[...] = total.astype(BF16)
    rzl[me_z] = szl[me_z]

    def send_zl(d):
        z, device = at_z(d)
        send(szl.at[z], rzl.at[me_z], 17, device)

    loop(1, NZ, send_zl)

    dr = jnp.zeros((256, 128), F32)
    for jg in range(4):
        dr = dr + jnp.where(group == jg, nt(bp[jg], w4[...]), 0.0)
    drf[...] = dr * (1.0 / 16.0)
    for s in range(16):
        sdr[s // 2, (s % 2) * 16 : (s % 2) * 16 + 16, :] = drf[pl.ds(s, 16, stride=16), :].astype(BF16)
    rdr[me_q] = sdr[me_q]

    def send_dr(d):
        q, device = at_q(d)
        send(sdr.at[q], rdr.at[me_q], 5, device)

    loop(1, NQ, send_dr)

    def make_gw(n):
        lanes = pl.ds(pl.multiple_of(lax.rem(n + 2 - 2 * core, 4) * 1024, 1024), 1024)
        gwp[:, lanes] = nn(rl[...], bp[:, :, lanes].reshape(1024, 1024))

        @pl.when(n == 1)
        def _():
            sgc[...] = gwp[:, pl.ds(pl.multiple_of((1 - core) * 2048, 2048), 2048)].astype(BF16)
            send(sgc, rgc, 6, mate)

    loop(0, 4, make_gw)

    arrived(rgc, 6)
    for p in range(16):
        lanes = pl.ds(pl.multiple_of(core * 2048 + p * 128, 128), 128)
        half = gwp[:, lanes] + rgc[:, p * 128 : (p + 1) * 128].astype(F32)
        sgx[p] = half.astype(BF16)
    rgx[me_p] = sgx[me_p]

    def send_gx(d):
        p, device = at_p(d)
        send(sgx.at[p], rgx.at[me_p], 7, device)

    loop(1, NXY, send_gx)

    def tiled(v, first):
        for n in range(8):
            ssm[first + n] = v[n // 2 * 8 : n // 2 * 8 + 8, n % 2 * 128 : n % 2 * 128 + 128]

    arrived(rzl.at[pl.ds(0, NZ - 1)], 17)
    dsum = rzl[0].astype(F32)
    for z in range(1, NZ):
        dsum = dsum + rzl[z].astype(F32)
    dsum = dsum.astype(BF16).astype(F32)
    parts = []
    for i3 in range(3):
        row = jnp.concatenate([dsum[i3 * 4 + cq : i3 * 4 + cq + 1, :] for cq in range(4)], axis=1)
        parts.append(jnp.where(lane_s, jnp.broadcast_to(row, (16, 512)), 0.0))
    dleft = nt(jnp.concatenate(parts, axis=0).astype(BF16), fold)
    hat = hat_r[...]
    tiled(nn(dleft.T[0:32, :].astype(BF16), hat.astype(BF16)), 0)
    back = nn(dleft[:, 0:32].astype(BF16), w1_ref[...])
    out = norm_back(back, hat, inv_r[:, 0:1])
    grows_ref[...] = out.reshape(3, 16, 256).astype(BF16)
    store_rows = fetch(grows_ref, grows_hbm, 7)

    arrived(bxy.at[pl.ds(0, NXY - 1)], 4)
    total = bxy[0]
    for p in range(1, NXY):
        total = total + bxy[p]
    bz[me_z] = total
    loop(1, NZ, lambda d: send(bz.at[me_z], bz.at[me_z], 8, at_z(d)[1]))

    arrived(rdr.at[pl.ds(0, NQ - 1)], 5)
    dsum = rdr[0].astype(F32)
    for q in range(1, NQ):
        dsum = dsum + rdr[q].astype(F32)
    dsum = dsum.astype(BF16).astype(F32)
    parts = []
    for t in range(2):
        for jg in range(4):
            parts.append(jnp.where(lane_group == jg, dsum[t * 16 : t * 16 + 16, :], 0.0))
    dright = jnp.concatenate(parts, axis=0)
    hat = hat_c[...]
    term = nn(dright.T.astype(BF16), hat.astype(BF16))
    term = term[0:32, :] + term[32:64, :] + term[64:96, :] + term[96:128, :]
    tiled(term, 8)
    rsx[me_p] = ssm[me_p]

    def send_small(d):
        p, device = at_p(d)
        send(ssm.at[p], rsx.at[me_p], 9, device)

    loop(1, NXY, send_small)
    back = nn(dright.astype(BF16), w2r[...])
    out = norm_back(back, hat, inv_c[:, 0:1])
    gcols_ref[...] = out.reshape(2, 64, 256).astype(BF16)
    store_cols = fetch(gcols_ref, gcols_hbm, 8)

    def make_p(jg):
        for p in range(8):
            lanes = pl.ds(pl.multiple_of(jg * 2048 + p * 256, 256), 256)
            r = nn(lm[...], ap[:, lanes])
            for h in range(2):
                pf[pl.ds(jg * 16 + 2 * p + h, 96, stride=64), :] = r[:, h * 128 : (h + 1) * 128]

    loop(0, 4, make_p)

    load_b.wait()
    bias = b_ref[...]

    def finish(n):
        for u in range(4):
            rows = pf[pl.ds(pl.multiple_of((4 * n + u) * 64, 64), 64), :]
            po[4 * n + u] = (rows + bias).astype(BF16)

    loop(0, 24, finish)
    store_pair = fetch(po, pair_hbm, 9)

    arrived(rgx.at[pl.ds(0, NXY - 1)], 7)
    total = rgx[0].astype(F32)
    for p in range(1, NXY):
        total = total + rgx[p].astype(F32)
    rgz[me_z] = total.astype(BF16)
    loop(1, NZ, lambda d: send(rgz.at[me_z], rgz.at[me_z], 11, at_z(d)[1]))

    arrived(rsx.at[pl.ds(0, NXY - 1)], 9)
    total = rsx[0]
    for p in range(1, NXY):
        total = total + rsx[p]
    rsz[me_w] = total
    loop(1, NW, lambda d: send(rsz.at[me_w], rsz.at[me_w], 10, at_zc(d)[1]))

    arrived(rgz.at[pl.ds(0, NZ - 1)], 11)
    total = rgz[0].astype(F32)
    for z in range(1, NZ):
        total = total + rgz[z].astype(F32)
    fgw[core, me_p] = total.astype(BF16)
    loop(1, NXY, lambda d: send(fgw.at[core, me_p], fgw.at[core, me_p], 13, at_p(d)[1]))

    arrived(rsz.at[pl.ds(0, NW - 1)], 10)
    total = rsz[0]
    for w in range(1, NW):
        total = total + rsz[w]
    fsm[me_p] = total
    loop(1, NXY, lambda d: send(fsm.at[me_p], fsm.at[me_p], 14, at_p(d)[1]))

    arrived(bz.at[pl.ds(0, NZ - 1)], 8)
    total = bz[0]
    for z in range(1, NZ):
        total = total + bz[z]
    gb_ref[...] = total[0:1, :]
    store_b = fetch(gb_ref, gb_hbm, 10)

    arrived(fgw.at[0, pl.ds(0, NXY - 1)], 13)
    send(fgw.at[core], fgw.at[core], 15, mate)
    mine = pl.ds(pl.multiple_of(core * 512, 512), 512)
    gw_ref[mine, :] = fgw[core].astype(F32).reshape(512, 128)
    store_mine = fetch(gw_ref.at[mine], gw_hbm.at[mine], 15)
    arrived(fsm.at[pl.ds(0, NXY - 1)], 14)
    for n in range(16):
        gsm_ref[n // 8, n % 8 // 2 * 8 : n % 8 // 2 * 8 + 8, n % 2 * 128 : n % 2 * 128 + 128] = fsm[n]
    store_wl = fetch(gsm_ref.at[0], gwl_hbm, 11)
    store_wr = fetch(gsm_ref.at[1], gwr_hbm, 12)
    arrived(fgw.at[0], 15)
    other = pl.ds(pl.multiple_of((1 - core) * 512, 512), 512)
    gw_ref[other, :] = fgw[1 - core].astype(F32).reshape(512, 128)
    store_other = fetch(gw_ref.at[other], gw_hbm.at[other], 16)

    for copy in (store_rows, store_cols, store_pair, store_b, store_mine, store_other, store_wl, store_wr):
        copy.wait()
    sent(rbuf.at[pl.ds(0, NQ - 1)], 0)
    sent(lbuf.at[0, pl.ds(0, NZ - 1)], 1)
    sent(bsend, 2)
    sent(rdl.at[pl.ds(0, NC - 1)], 3)
    sent(bxy.at[pl.ds(0, NXY - 1)], 4)
    sent(rdr.at[pl.ds(0, NQ - 1)], 5)
    sent(rgc, 6)
    sent(rgx.at[pl.ds(0, NXY - 1)], 7)
    sent(bz.at[pl.ds(0, NZ - 1)], 8)
    sent(rsx.at[pl.ds(0, NXY - 1)], 9)
    sent(rsz.at[pl.ds(0, NW - 1)], 10)
    sent(rgz.at[pl.ds(0, NZ - 1)], 11)
    sent(fgw.at[0, pl.ds(0, NXY - 1)], 13)
    sent(fsm.at[pl.ds(0, NXY - 1)], 14)
    sent(fgw.at[0], 15)
    sent(lbuf.at[pl.ds(0, NC - 1)], 16)
    sent(rzl.at[pl.ds(0, NZ - 1)], 17)


SCRATCH = (
    ((3, 16, 256), BF16),
    ((2, 64, 256), BF16),
    ((32, 256), BF16),
    ((32, 256), BF16),
    ((1024, 128), BF16),
    ((1, 128), F32),
    ((3, 16, 256), BF16),
    ((2, 64, 256), BF16),
    ((1024, 128), F32),
    ((1, 128), F32),
    ((96, 64, 128), BF16),
    ((96, 8192), BF16),
    ((6144, 128), F32),
    ((96, 64, 128), BF16),
    ((128, 4096), BF16),
    ((128, 256), BF16),
    ((48, 256), F32),
    ((128, 256), F32),
    ((48, 128), F32),
    ((128, 128), F32),
    ((256, 128), F32),
    ((1024, 128), BF16),
    ((32, 1024), BF16),
    ((512, 8192), BF16),
    ((4, 256, 4096), BF16),
    ((512, 128), F32),
    ((4, 96, 128), F32),
    ((96, 512), BF16),
    ((512, 96), BF16),
    ((4, 96, 128), F32),
    ((512, 128), F32),
    ((256, 128), F32),
    ((32, 4096), F32),
    ((NQ, 32, 128), BF16),
    ((NC, NZ, 16, 128), BF16),
    ((NC, NZ, 16, 128), BF16),
    ((NC, NZ, 16, 128), BF16),
    ((NZ, 16, 128), BF16),
    ((NZ, 16, 128), BF16),
    ((NQ, 32, 128), BF16),
    ((NQ, 32, 128), BF16),
    ((8, 128), F32),
    ((8, 128), F32),
    ((NXY, 8, 128), F32),
    ((NZ, 8, 128), F32),
    ((32, 2048), BF16),
    ((32, 2048), BF16),
    ((NXY, 32, 128), BF16),
    ((NXY, 32, 128), BF16),
    ((NZ, 32, 128), BF16),
    ((2, NXY, 32, 128), BF16),
    ((NXY, 8, 128), F32),
    ((NXY, 8, 128), F32),
    ((NW, 8, 128), F32),
    ((NXY, 8, 128), F32),
    ((2, 32, 256), F32),
)
SENDS = 18


OUTS = (
    ((96, 64, 128), BF16),
    ((3, 16, 256), BF16),
    ((2, 64, 256), BF16),
    ((1024, 128), F32),
    ((1, 128), F32),
    ((32, 256), F32),
    ((32, 256), F32),
)


def hand_over(*refs):
    n = len(OUTS)
    given, taken, held, insem, outsem = refs[:n], refs[n : 2 * n], refs[2 * n : 3 * n], refs[-2], refs[-1]
    pieces = [(0, pl.ds(k * 24, 24)) for k in range(4)] + [(k, None) for k in range(1, n)]
    loads, stores = [], []
    for m, (k, part) in enumerate(pieces):
        source, slot, target = (r[k] if part is None else r[k].at[part] for r in (given, held, taken))
        loads.append(pltpu.make_async_copy(source, slot, insem.at[m]))
        stores.append(pltpu.make_async_copy(slot, target, outsem.at[m]))
    for load in loads:
        load.start()
    for load, store in zip(loads, stores):
        load.wait()
        store.start()
    for store in stores:
        store.wait()


def local(xs, xc, w1, w2, w, b, g):
    hbm = pl.BlockSpec(memory_space=pl.ANY)
    outs = tuple(jax.ShapeDtypeStruct(shape, dtype) for shape, dtype in OUTS)
    found = pl.pallas_call(
        kernel,
        out_shape=outs,
        in_specs=[hbm] * 7,
        out_specs=(hbm,) * 7,
        scratch_shapes=[pltpu.VMEM(shape, dtype) for shape, dtype in SCRATCH]
        + [pltpu.SemaphoreType.DMA((17,))]
        + [pltpu.SemaphoreType.DMA((SENDS,))] * 2,
        compiler_params=pltpu.CompilerParams(
            collective_id=0, has_side_effects=True, vmem_limit_bytes=56 << 20
        ),
        cost_estimate=pl.CostEstimate(flops=3_300_000_000, bytes_accessed=5_000_000, transcendentals=0),
    )(jnp.transpose(xs, (1, 0, 2)), xc, w1.T, w2.T, w, b.reshape(1, 128), g)
    pair, grows, gcols, gw, gb, gwl, gwr = pl.pallas_call(
        hand_over,
        out_shape=outs,
        in_specs=[hbm] * 7,
        out_specs=(hbm,) * 7,
        scratch_shapes=[pltpu.VMEM(shape, dtype) for shape, dtype in OUTS]
        + [pltpu.SemaphoreType.DMA((len(OUTS) + 3,))] * 2,
    )(*found)
    return pair, jnp.transpose(grows, (1, 0, 2)), gcols, gw, gb.reshape(128), gwl.T, gwr.T


def solution(mesh):
    return jax.shard_map(
        local,
        mesh=mesh,
        in_specs=(
            P(None, ("qrow", "kcol"), None),
            P("qrow", "kcol", None),
            P(),
            P(),
            P(),
            P(),
            P("qrow", "kcol", None),
        ),
        out_specs=(
            P("qrow", "kcol", None),
            P(None, ("qrow", "kcol"), None),
            P("qrow", "kcol", None),
            P(),
            P(),
            P(),
            P(),
        ),
        check_vma=False,
    )
```

```python
import jax
import jax.numpy as jnp
from jax import lax
from jax.experimental import pallas as pl
from jax.experimental.pallas import tpu as pltpu
from jax.sharding import PartitionSpec as P

F32, BF16 = jnp.float32, jnp.bfloat16
MESH = pl.DeviceIdType.MESH
EPS = 1e-05

NQ, NZ, NC, NXY, NW = 8, 8, 4, 16, 16


def nn(a, b):
    return jnp.dot(a, b, preferred_element_type=F32)


def nt(a, b):
    return lax.dot_general(a, b, (((1,), (1,)), ((), ())), preferred_element_type=F32)


def mean_of(v):
    return jnp.mean(v, axis=-1, keepdims=True)


def normalize(v):
    center = v - mean_of(v)
    inv = lax.rsqrt(mean_of(center * center) + EPS)
    return center * inv, inv


def norm_back(g, hat, inv):
    return inv * (g - mean_of(g) - hat * mean_of(g * hat))


def iota(shape, dim):
    return lax.broadcasted_iota(jnp.int32, shape, dim)


def loop(lo, hi, body):
    def step(d, carry):
        body(d)
        return carry

    lax.fori_loop(lo, hi, step, 0)


def kernel(
    xs_hbm, xc_hbm, w1_hbm, w2_hbm, w_hbm, b_hbm, g_hbm,
    pair_hbm, grows_hbm, gcols_hbm, gw_hbm, gb_hbm, gwl_hbm, gwr_hbm,
    xs_ref, xc_ref, w1_ref, w2_ref, w_ref, b_ref, grows_ref, gcols_ref, gw_ref, gb_ref,
    g, gs, pf, po, w4, w2r, hat_r, hat_c, inv_r, inv_c,
    rf, rm, rl, ap, bp, lf, lmf, lm, lt, dlf, dsf, drf, gwp,
    rbuf, lbuf, sdl, rdl, szl, rzl, sdr, rdr,
    bsend, bcore, bxy, bz,
    sgc, rgc, sgx, rgx, rgz, fgw,
    ssm, rsx, rsz, fsm, gsm_ref,
    lsem, ssem, rsem,
):
    me_q, me_k = lax.axis_index("qrow"), lax.axis_index("kcol")
    me_z = lax.div(me_k, 4)
    me_x = lax.rem(lax.div(me_k, 2), 2)
    core = lax.rem(me_k, 2)
    me_p = me_x * 8 + me_q
    me_c = me_x * 2 + core
    me_w = me_z * 2 + core

    def at_c(d):
        c = lax.rem(me_c + d, NC)
        return c, (me_q, me_z * 4 + c)

    def at_q(d):
        q = lax.rem(me_q + d, NQ)
        return q, (q, me_k)

    def at_p(d):
        p = lax.rem(me_p + d, NXY)
        return p, (lax.rem(p, 8), me_z * 4 + lax.div(p, 8) * 2 + core)

    def at_z(d):
        z = lax.rem(me_z + d, NZ)
        return z, (me_q, z * 4 + me_x * 2 + core)

    def at_zc(d):
        w = lax.rem(me_w + d, NW)
        return w, (me_q, lax.div(w, 2) * 4 + me_x * 2 + lax.rem(w, 2))

    mate = (me_q, me_k + 1 - 2 * core)

    def send(src, dst, n, device):
        pltpu.make_async_remote_copy(
            src_ref=src, dst_ref=dst, send_sem=ssem.at[n], recv_sem=rsem.at[n],
            device_id=device, device_id_type=MESH,
        ).start()

    def arrived(ref, n):
        pltpu.make_async_copy(ref, ref, rsem.at[n]).wait()

    def sent(ref, n):
        pltpu.make_async_copy(ref, ref, ssem.at[n]).wait()

    def fetch(src, dst, n):
        copy = pltpu.make_async_copy(src, dst, lsem.at[n])
        copy.start()
        return copy

    load_xc = fetch(xc_hbm, xc_ref, 0)
    load_w2 = fetch(w2_hbm, w2_ref, 1)
    load_xs = fetch(xs_hbm, xs_ref, 2)
    load_w1 = fetch(w1_hbm, w1_ref, 3)
    load_g = fetch(g_hbm, g, 4)
    load_w = fetch(w_hbm, w_ref, 5)
    load_b = fetch(b_hbm, b_ref, 6)

    barrier = pltpu.get_barrier_semaphore()

    def greet(device):
        pl.semaphore_signal(barrier, inc=1, device_id=device, device_id_type=MESH)

    loop(1, NW, lambda d: greet(at_zc(d)[1]))
    loop(1, NXY, lambda d: greet(at_p(d)[1]))
    greet((me_q, me_z * 4 + 3 - me_c))

    lane_group = lax.shift_right_logical(iota((16, 128), 1), 5)
    lane_s = jnp.bitwise_and(iota((16, 512), 1), 15) == iota((16, 512), 0)
    fold = (lax.shift_right_logical(iota((128, 512), 1), 4) == iota((128, 512), 0)).astype(BF16)

    load_xc.wait()
    load_w2.wait()
    for jg in range(4):
        w2r[jg * 32 : (jg + 1) * 32, :] = w2_ref[...]
    hat, inv = normalize(xc_ref[...].astype(F32).reshape(128, 256))
    hat_c[...] = hat
    inv_c[...] = jnp.broadcast_to(inv, (128, 128))
    right = nt(hat.astype(BF16), w2r[...]).astype(BF16).astype(F32)
    tiles = []
    for t in range(2):
        tile = right[t * 64 : t * 64 + 16, :]
        for jg in range(1, 4):
            tile = jnp.where(lane_group == jg, right[t * 64 + jg * 16 : t * 64 + jg * 16 + 16, :], tile)
        tiles.append(tile)
    rbuf[me_q] = jnp.concatenate(tiles, axis=0).astype(BF16)

    pl.semaphore_wait(barrier, NW + NXY - 1)
    loop(1, NQ, lambda d: send(rbuf.at[me_q], rbuf.at[me_q], 0, at_q(d)[1]))

    load_xs.wait()
    load_w1.wait()
    hat, inv = normalize(xs_ref[...].astype(F32).reshape(48, 256))
    hat_r[...] = hat
    inv_r[...] = jnp.broadcast_to(inv, (48, 128))
    left = nt(hat.astype(BF16), w1_ref[...]).astype(BF16)
    tile = jnp.zeros((16, 128), F32)
    for i3 in range(3):
        wide = nn(left[i3 * 16 : i3 * 16 + 16, :], fold[0:32, :])
        row = jnp.sum(jnp.where(lane_s, wide, 0.0), axis=0, keepdims=True)
        for cq in range(4):
            piece = jnp.broadcast_to(row[:, cq * 128 : (cq + 1) * 128], (16, 128))
            tile = jnp.where(iota((16, 128), 0) == i3 * 4 + cq, piece, tile)
    lbuf[me_c, me_z] = tile.astype(BF16)

    loop(1, NZ, lambda d: send(lbuf.at[me_c, me_z], lbuf.at[me_c, me_z], 1, at_z(d)[1]))

    load_w.wait()
    for c in range(32):
        block = w_ref[c * 32 : (c + 1) * 32, :]
        for jg in range(4):
            w4[jg * 32 : (jg + 1) * 32, c * 128 : (c + 1) * 128] = block

    load_g.wait()

    def widen(n, total):
        for u in range(4):
            v = g[4 * n + u].astype(F32)
            pf[pl.ds(pl.multiple_of((4 * n + u) * 64, 64), 64), :] = v
            total = total + v
        return total

    total = lax.fori_loop(0, 24, widen, jnp.zeros((64, 128), F32))
    bsend[...] = jnp.broadcast_to(jnp.sum(total, axis=0, keepdims=True), (8, 128))

    def turn(n):
        for u in range(4):
            lanes = pl.ds(pl.multiple_of((4 * n + u) * 128, 128), 128)
            gs[:, lanes] = pf[pl.ds(4 * n + u, 96, stride=64), :].astype(BF16)

    loop(0, 16, turn)
    send(bsend, bcore, 2, mate)

    arrived(rbuf.at[pl.ds(0, NQ - 1)], 0)
    for s in range(16):
        part = rbuf[s // 2, (s % 2) * 16 : (s % 2) * 16 + 16, :].astype(F32)
        rf[pl.ds(s, 16, stride=16), :] = part * (1.0 / 16.0)
    rx = rf[...]
    group = lax.shift_right_logical(iota((256, 128), 1), 5)
    for jg in range(4):
        rm[jg * 256 : (jg + 1) * 256, :] = jnp.where(group == jg, rx, 0.0).astype(BF16)
    rxt = rx.T
    for jg in range(4):
        rl[:, jg * 256 : (jg + 1) * 256] = rxt[jg * 32 : (jg + 1) * 32, :].astype(BF16)

    def make_a(n):
        @pl.when(n == 1)
        def _():
            arrived(lbuf.at[0, pl.ds(0, NZ - 1)], 1)
            loop(1, NC, lambda d: send(lbuf.at[me_c], lbuf.at[me_c], 16, at_c(d)[1]))

        for u in range(2):
            jg = 2 * n + u
            for cc in range(16):
                r = nn(
                    rm[pl.ds(pl.multiple_of(jg * 256, 256), 256), :],
                    w4[:, cc * 256 : (cc + 1) * 256],
                ).astype(BF16)
                for j in range(16):
                    lanes = pl.ds(pl.multiple_of((jg * 16 + j) * 128, 128), 128)
                    for h in range(2):
                        to = cc * 32 + h * 16
                        ap[to : to + 16, lanes] = r[j * 16 : (j + 1) * 16, h * 128 : (h + 1) * 128]

    loop(0, 2, make_a)

    dl = nt(ap[...], gs[...])
    for cq in range(4):
        dlf[cq] = dl[cq * 128 : (cq + 1) * 128, :].T
    dsf[...] = jnp.zeros((512, 128), F32)
    for c in range(4):
        for i3 in range(3):
            for cq in range(4):
                part = dlf[cq, pl.ds(c * 3 + i3, 8, stride=12), :]
                dsf[pl.ds(c * 128 + i3 * 4 + cq, 8, stride=16), :] = part
    sdl[...] = dsf[...].astype(BF16).reshape(4, 8, 16, 128)
    rdl[me_c] = sdl[me_c]

    def send_dl(d):
        c, device = at_c(d)
        send(sdl.at[c], rdl.at[me_c], 3, device)

    loop(1, NC, send_dl)

    arrived(lbuf.at[pl.ds(0, NC - 1)], 16)
    lf[...] = lbuf[...].astype(F32).reshape(512, 128)
    for c in range(4):
        for i3 in range(3):
            for cq in range(4):
                part = lf[pl.ds(c * 128 + i3 * 4 + cq, 8, stride=16), :]
                lmf[cq, pl.ds(c * 3 + i3, 8, stride=12), :] = part
    for cq in range(4):
        lm[:, cq * 128 : (cq + 1) * 128] = lmf[cq].astype(BF16)
        lt[cq * 128 : (cq + 1) * 128, :] = lmf[cq].T.astype(BF16)

    arrived(bcore, 2)
    bxy[me_p] = bsend[...] + bcore[...]
    loop(1, NXY, lambda d: send(bxy.at[me_p], bxy.at[me_p], 4, at_p(d)[1]))

    def make_b(n):
        for u in range(2):
            jg = 2 * n + u
            for p in range(8):
                lanes = pl.ds(pl.multiple_of(jg * 2048 + p * 256, 256), 256)
                r = nn(lt[...], gs[:, lanes]).astype(BF16)
                for c in range(32):
                    for h in range(2):
                        to = (p * 2 + h) * 16
                        bp[jg, to : to + 16, c * 128 : (c + 1) * 128] = r[c * 16 : (c + 1) * 16, h * 128 : (h + 1) * 128]

    loop(0, 2, make_b)

    arrived(rdl.at[pl.ds(0, NC - 1)], 3)
    total = rdl[0].astype(F32)
    for c in range(1, NC):
        total = total + rdl[c].astype(F32)
    szl[...] = total.astype(BF16)
    rzl[me_z] = szl[me_z]

    def send_zl(d):
        z, device = at_z(d)
        send(szl.at[z], rzl.at[me_z], 17, device)

    loop(1, NZ, send_zl)

    dr = jnp.zeros((256, 128), F32)
    for jg in range(4):
        dr = dr + jnp.where(group == jg, nt(bp[jg], w4[...]), 0.0)
    drf[...] = dr * (1.0 / 16.0)
    for s in range(16):
        sdr[s // 2, (s % 2) * 16 : (s % 2) * 16 + 16, :] = drf[pl.ds(s, 16, stride=16), :].astype(BF16)
    rdr[me_q] = sdr[me_q]

    def send_dr(d):
        q, device = at_q(d)
        send(sdr.at[q], rdr.at[me_q], 5, device)

    loop(1, NQ, send_dr)

    def make_gw(n):
        lanes = pl.ds(pl.multiple_of(lax.rem(n + 2 - 2 * core, 4) * 1024, 1024), 1024)
        gwp[:, lanes] = nn(rl[...], bp[:, :, lanes].reshape(1024, 1024))

        @pl.when(n == 1)
        def _():
            sgc[...] = gwp[:, pl.ds(pl.multiple_of((1 - core) * 2048, 2048), 2048)].astype(BF16)
            send(sgc, rgc, 6, mate)

    loop(0, 4, make_gw)

    arrived(rgc, 6)
    for p in range(16):
        lanes = pl.ds(pl.multiple_of(core * 2048 + p * 128, 128), 128)
        half = gwp[:, lanes] + rgc[:, p * 128 : (p + 1) * 128].astype(F32)
        sgx[p] = half.astype(BF16)
    rgx[me_p] = sgx[me_p]

    def send_gx(d):
        p, device = at_p(d)
        send(sgx.at[p], rgx.at[me_p], 7, device)

    loop(1, NXY, send_gx)

    def tiled(v, first):
        for n in range(8):
            ssm[first + n] = v[n // 2 * 8 : n // 2 * 8 + 8, n % 2 * 128 : n % 2 * 128 + 128]

    arrived(rzl.at[pl.ds(0, NZ - 1)], 17)
    dsum = rzl[0].astype(F32)
    for z in range(1, NZ):
        dsum = dsum + rzl[z].astype(F32)
    dsum = dsum.astype(BF16).astype(F32)
    parts = []
    for i3 in range(3):
        row = jnp.concatenate([dsum[i3 * 4 + cq : i3 * 4 + cq + 1, :] for cq in range(4)], axis=1)
        parts.append(jnp.where(lane_s, jnp.broadcast_to(row, (16, 512)), 0.0))
    dleft = nt(jnp.concatenate(parts, axis=0).astype(BF16), fold)
    hat = hat_r[...]
    tiled(nn(dleft.T[0:32, :].astype(BF16), hat.astype(BF16)), 0)
    back = nn(dleft[:, 0:32].astype(BF16), w1_ref[...])
    out = norm_back(back, hat, inv_r[:, 0:1])
    grows_ref[...] = out.reshape(3, 16, 256).astype(BF16)
    store_rows = fetch(grows_ref, grows_hbm, 7)

    arrived(bxy.at[pl.ds(0, NXY - 1)], 4)
    total = bxy[0]
    for p in range(1, NXY):
        total = total + bxy[p]
    bz[me_z] = total
    loop(1, NZ, lambda d: send(bz.at[me_z], bz.at[me_z], 8, at_z(d)[1]))

    arrived(rdr.at[pl.ds(0, NQ - 1)], 5)
    dsum = rdr[0].astype(F32)
    for q in range(1, NQ):
        dsum = dsum + rdr[q].astype(F32)
    dsum = dsum.astype(BF16).astype(F32)
    parts = []
    for t in range(2):
        for jg in range(4):
            parts.append(jnp.where(lane_group == jg, dsum[t * 16 : t * 16 + 16, :], 0.0))
    dright = jnp.concatenate(parts, axis=0)
    hat = hat_c[...]
    term = nn(dright.T.astype(BF16), hat.astype(BF16))
    term = term[0:32, :] + term[32:64, :] + term[64:96, :] + term[96:128, :]
    tiled(term, 8)
    rsx[me_p] = ssm[me_p]

    def send_small(d):
        p, device = at_p(d)
        send(ssm.at[p], rsx.at[me_p], 9, device)

    loop(1, NXY, send_small)
    back = nn(dright.astype(BF16), w2r[...])
    out = norm_back(back, hat, inv_c[:, 0:1])
    gcols_ref[...] = out.reshape(2, 64, 256).astype(BF16)
    store_cols = fetch(gcols_ref, gcols_hbm, 8)

    def make_p(jg):
        for p in range(8):
            lanes = pl.ds(pl.multiple_of(jg * 2048 + p * 256, 256), 256)
            r = nn(lm[...], ap[:, lanes])
            for h in range(2):
                pf[pl.ds(jg * 16 + 2 * p + h, 96, stride=64), :] = r[:, h * 128 : (h + 1) * 128]

    loop(0, 4, make_p)

    load_b.wait()
    bias = b_ref[...]

    def finish(n):
        for u in range(4):
            rows = pf[pl.ds(pl.multiple_of((4 * n + u) * 64, 64), 64), :]
            po[4 * n + u] = (rows + bias).astype(BF16)

    loop(0, 24, finish)
    store_pair = fetch(po, pair_hbm, 9)

    arrived(rgx.at[pl.ds(0, NXY - 1)], 7)
    total = rgx[0].astype(F32)
    for p in range(1, NXY):
        total = total + rgx[p].astype(F32)
    rgz[me_z] = total.astype(BF16)
    loop(1, NZ, lambda d: send(rgz.at[me_z], rgz.at[me_z], 11, at_z(d)[1]))

    arrived(rsx.at[pl.ds(0, NXY - 1)], 9)
    total = rsx[0]
    for p in range(1, NXY):
        total = total + rsx[p]
    rsz[me_w] = total
    loop(1, NW, lambda d: send(rsz.at[me_w], rsz.at[me_w], 10, at_zc(d)[1]))

    arrived(rgz.at[pl.ds(0, NZ - 1)], 11)
    total = rgz[0].astype(F32)
    for z in range(1, NZ):
        total = total + rgz[z].astype(F32)
    fgw[core, me_p] = total.astype(BF16)
    loop(1, NXY, lambda d: send(fgw.at[core, me_p], fgw.at[core, me_p], 13, at_p(d)[1]))

    arrived(rsz.at[pl.ds(0, NW - 1)], 10)
    total = rsz[0]
    for w in range(1, NW):
        total = total + rsz[w]
    fsm[me_p] = total
    loop(1, NXY, lambda d: send(fsm.at[me_p], fsm.at[me_p], 14, at_p(d)[1]))

    arrived(bz.at[pl.ds(0, NZ - 1)], 8)
    total = bz[0]
    for z in range(1, NZ):
        total = total + bz[z]
    gb_ref[...] = total[0:1, :]
    store_b = fetch(gb_ref, gb_hbm, 10)

    arrived(fgw.at[0, pl.ds(0, NXY - 1)], 13)
    send(fgw.at[core], fgw.at[core], 15, mate)
    mine = pl.ds(pl.multiple_of(core * 512, 512), 512)
    gw_ref[mine, :] = fgw[core].astype(F32).reshape(512, 128)
    store_mine = fetch(gw_ref.at[mine], gw_hbm.at[mine], 15)
    arrived(fsm.at[pl.ds(0, NXY - 1)], 14)
    for n in range(16):
        gsm_ref[n // 8, n % 8 // 2 * 8 : n % 8 // 2 * 8 + 8, n % 2 * 128 : n % 2 * 128 + 128] = fsm[n]
    store_wl = fetch(gsm_ref.at[0], gwl_hbm, 11)
    store_wr = fetch(gsm_ref.at[1], gwr_hbm, 12)
    arrived(fgw.at[0], 15)
    other = pl.ds(pl.multiple_of((1 - core) * 512, 512), 512)
    gw_ref[other, :] = fgw[1 - core].astype(F32).reshape(512, 128)
    store_other = fetch(gw_ref.at[other], gw_hbm.at[other], 16)

    for copy in (store_rows, store_cols, store_pair, store_b, store_mine, store_other, store_wl, store_wr):
        copy.wait()
    sent(rbuf.at[pl.ds(0, NQ - 1)], 0)
    sent(lbuf.at[0, pl.ds(0, NZ - 1)], 1)
    sent(bsend, 2)
    sent(rdl.at[pl.ds(0, NC - 1)], 3)
    sent(bxy.at[pl.ds(0, NXY - 1)], 4)
    sent(rdr.at[pl.ds(0, NQ - 1)], 5)
    sent(rgc, 6)
    sent(rgx.at[pl.ds(0, NXY - 1)], 7)
    sent(bz.at[pl.ds(0, NZ - 1)], 8)
    sent(rsx.at[pl.ds(0, NXY - 1)], 9)
    sent(rsz.at[pl.ds(0, NW - 1)], 10)
    sent(rgz.at[pl.ds(0, NZ - 1)], 11)
    sent(fgw.at[0, pl.ds(0, NXY - 1)], 13)
    sent(fsm.at[pl.ds(0, NXY - 1)], 14)
    sent(fgw.at[0], 15)
    sent(lbuf.at[pl.ds(0, NC - 1)], 16)
    sent(rzl.at[pl.ds(0, NZ - 1)], 17)


SCRATCH = (
    ((3, 16, 256), BF16),
    ((2, 64, 256), BF16),
    ((32, 256), BF16),
    ((32, 256), BF16),
    ((1024, 128), BF16),
    ((1, 128), F32),
    ((3, 16, 256), BF16),
    ((2, 64, 256), BF16),
    ((1024, 128), F32),
    ((1, 128), F32),
    ((96, 64, 128), BF16),
    ((96, 8192), BF16),
    ((6144, 128), F32),
    ((96, 64, 128), BF16),
    ((128, 4096), BF16),
    ((128, 256), BF16),
    ((48, 256), F32),
    ((128, 256), F32),
    ((48, 128), F32),
    ((128, 128), F32),
    ((256, 128), F32),
    ((1024, 128), BF16),
    ((32, 1024), BF16),
    ((512, 8192), BF16),
    ((4, 256, 4096), BF16),
    ((512, 128), F32),
    ((4, 96, 128), F32),
    ((96, 512), BF16),
    ((512, 96), BF16),
    ((4, 96, 128), F32),
    ((512, 128), F32),
    ((256, 128), F32),
    ((32, 4096), F32),
    ((NQ, 32, 128), BF16),
    ((NC, NZ, 16, 128), BF16),
    ((NC, NZ, 16, 128), BF16),
    ((NC, NZ, 16, 128), BF16),
    ((NZ, 16, 128), BF16),
    ((NZ, 16, 128), BF16),
    ((NQ, 32, 128), BF16),
    ((NQ, 32, 128), BF16),
    ((8, 128), F32),
    ((8, 128), F32),
    ((NXY, 8, 128), F32),
    ((NZ, 8, 128), F32),
    ((32, 2048), BF16),
    ((32, 2048), BF16),
    ((NXY, 32, 128), BF16),
    ((NXY, 32, 128), BF16),
    ((NZ, 32, 128), BF16),
    ((2, NXY, 32, 128), BF16),
    ((NXY, 8, 128), F32),
    ((NXY, 8, 128), F32),
    ((NW, 8, 128), F32),
    ((NXY, 8, 128), F32),
    ((2, 32, 256), F32),
)
SENDS = 18


OUTS = (
    ((96, 64, 128), BF16),
    ((3, 16, 256), BF16),
    ((2, 64, 256), BF16),
    ((1024, 128), F32),
    ((1, 128), F32),
    ((32, 256), F32),
    ((32, 256), F32),
)


def hand_over(*refs):
    n = len(OUTS)
    given, taken, held, insem, outsem = refs[:n], refs[n : 2 * n], refs[2 * n : 3 * n], refs[-2], refs[-1]
    pieces = [(0, pl.ds(k * 24, 24)) for k in range(4)] + [(k, None) for k in range(1, n)]
    loads, stores = [], []
    for m, (k, part) in enumerate(pieces):
        source, slot, target = (r[k] if part is None else r[k].at[part] for r in (given, held, taken))
        loads.append(pltpu.make_async_copy(source, slot, insem.at[m]))
        stores.append(pltpu.make_async_copy(slot, target, outsem.at[m]))
    for load in loads:
        load.start()
    for load, store in zip(loads, stores):
        load.wait()
        store.start()
    for store in stores:
        store.wait()


def local(xs, xc, w1, w2, w, b, g):
    hbm = pl.BlockSpec(memory_space=pl.ANY)
    outs = tuple(jax.ShapeDtypeStruct(shape, dtype) for shape, dtype in OUTS)
    found = pl.pallas_call(
        kernel,
        out_shape=outs,
        in_specs=[hbm] * 7,
        out_specs=(hbm,) * 7,
        scratch_shapes=[pltpu.VMEM(shape, dtype) for shape, dtype in SCRATCH]
        + [pltpu.SemaphoreType.DMA((17,))]
        + [pltpu.SemaphoreType.DMA((SENDS,))] * 2,
        compiler_params=pltpu.CompilerParams(
            collective_id=0, has_side_effects=True, vmem_limit_bytes=56 << 20
        ),
        cost_estimate=pl.CostEstimate(flops=3_300_000_000, bytes_accessed=5_000_000, transcendentals=0),
    )(jnp.transpose(xs, (1, 0, 2)), xc, w1.T, w2.T, w, b.reshape(1, 128), g)
    pair, grows, gcols, gw, gb, gwl, gwr = pl.pallas_call(
        hand_over,
        out_shape=outs,
        in_specs=[hbm] * 7,
        out_specs=(hbm,) * 7,
        scratch_shapes=[pltpu.VMEM(shape, dtype) for shape, dtype in OUTS]
        + [pltpu.SemaphoreType.DMA((len(OUTS) + 3,))] * 2,
    )(*found)
    return pair, jnp.transpose(grows, (1, 0, 2)), gcols, gw, gb.reshape(128), gwl.T, gwr.T


def solution(mesh):
    return jax.shard_map(
        local,
        mesh=mesh,
        in_specs=(
            P(None, ("qrow", "kcol"), None),
            P("qrow", "kcol", None),
            P(),
            P(),
            P(),
            P(),
            P("qrow", "kcol", None),
        ),
        out_specs=(
            P("qrow", "kcol", None),
            P(None, ("qrow", "kcol"), None),
            P("qrow", "kcol", None),
            P(),
            P(),
            P(),
            P(),
        ),
        check_vma=False,
    )
```
